256 devices in a mesh: rep: 16 (over y_hi, x, core), fsdp: 16 (over z, y_lo).
Axes of the slice: x: 4, y: 4 (y_hi: 2, y_lo: 2; y = y_hi * 2 + y_lo), z: 8, core: 2. Of those that a mesh axis runs over, the one named last changes fastest.
Arguments:
- tokens: bfloat16 [16, 8192, 3584], P('rep', 'fsdp'), may hold values from -6 to 6
- gain: float32 [3584], replicated, may hold values from 0.1 to 1.9
- cotangent: bfloat16 [16, 8192, 1024], P('rep', 'fsdp'), may hold values from -6 to 6
- params: float32 [16, 3584, 1024], P('rep', 'fsdp'), may hold values from -6 to 6
- momentum: float32 [16, 3584, 1024], P('rep', 'fsdp'), may hold values from -6 to 6
- step: int32 [1], replicated, may hold values from 0 to 2999
Outputs:
- keys: bfloat16 [16, 8192, 1024], P('rep', 'fsdp')
- input_gradient: bfloat16 [16, 8192, 3584], P('rep', 'fsdp')
- averaged: float32 [16, 3584, 1024], P('rep', 'fsdp')
- new_momentum: float32 [16, 3584, 1024], P('rep', 'fsdp')
The draws below stay inside these ranges and needn't reach their ends.
All inputs are finite; a program needn't handle non-finite values.
Results may differ from the reference program's by a relative error of at most 0.02.
Values may be sent and summed in bfloat16 or wider, within the bound.
No kernel may reach another device: no remote copies, remote signals or barrier semaphores. Data moves between devices by JAX's collectives and lax.ppermute only.
A program may use at most 128 MiB of HBM per device.

```python
import jax
import jax.numpy as jnp
from jax import lax

D = 3584
KW = 1024
TOK_REP = 8192
REPLICAS = 16


def block_levels(stream_key, extent, cuts, smallest, largest):
    level, own = 1.0, jax.random.fold_in(stream_key, 6)
    for position, blocks in cuts:
        steps = jnp.exp(jax.random.uniform(jax.random.fold_in(own, position), (blocks,), jnp.float32, smallest / len(cuts), largest / len(cuts)))
        level = level * jnp.repeat(steps, extent[position] // blocks).reshape([-1 if axis == position else 1 for axis in range(len(extent))])
    return level


def scatter_about(key, shape, width, limit, pieces=(), held_as=jnp.bfloat16):
    level = block_levels(key, shape, pieces, -0.22, 0.18) if pieces else 1.0
    entries = jax.random.normal(key, shape, jnp.float32) * width * level
    return jnp.minimum(jnp.maximum(entries, -limit), limit).astype(held_as)


def setup_inputs(seed: int = 0) -> dict:
    streams_of = jax.random.split(jax.random.key(seed), 7)
    tokens = scatter_about(streams_of[0], (REPLICAS, TOK_REP, D), 1.0, 6.0, ((0, 16), (1, 16)))
    gain = jnp.clip(1.0 + 0.18 * jax.random.normal(streams_of[1], (D,), jnp.float32), 0.1, 1.9)
    cotangent = scatter_about(streams_of[2], (REPLICAS, TOK_REP, KW), 1.0, 6.0, ((0, 16), (1, 16)))
    params = scatter_about(streams_of[3], (REPLICAS, D, KW), 1.0, 6.0, ((0, 16), (1, 16)), jnp.float32)
    momentum = scatter_about(streams_of[4], (REPLICAS, D, KW), 1.0, 6.0, ((0, 16), (1, 16)), jnp.float32)
    step = jax.random.randint(streams_of[5], (1,), 0, 3000).astype(jnp.int32)
    return {"tokens": tokens, "gain": gain, "cotangent": cotangent, "params": params, "momentum": momentum, "step": step}


BETA = 0.9
LRATE = 0.1
EPS = 1e-06

def reference(tokens, gain, cotangent, params, momentum, step):
    scale = D ** (-0.5)
    gain_vector = gain.astype(jnp.float32)

    def one_replica(items):
        x_in, cot, par, mom = items
        input_rows = x_in.astype(jnp.float32)
        root_mean_square = jnp.sqrt(lax.optimization_barrier(jnp.mean(input_rows * input_rows, axis=1, keepdims=True)) + EPS)
        input_hat = input_rows / root_mean_square
        normalized_input = (input_hat * gain_vector).astype(jnp.bfloat16)
        wb = par.astype(jnp.bfloat16)
        keys = (jnp.dot(normalized_input, wb, preferred_element_type=jnp.float32) * scale).astype(jnp.bfloat16)
        grad = jnp.dot(normalized_input.T, cot, preferred_element_type=jnp.float32) * scale
        dnormed = jnp.dot(cot, wb.T, preferred_element_type=jnp.float32) * scale
        incoming_gradient = dnormed * gain_vector
        inner_product = lax.optimization_barrier(jnp.mean(incoming_gradient * input_hat, axis=1, keepdims=True))
        input_gradient = ((incoming_gradient - input_hat * inner_product) / root_mean_square).astype(jnp.bfloat16)
        new_mom = BETA * mom + grad
        updated = par - LRATE * new_mom
        return (keys, input_gradient, updated, new_mom)
    keys, input_gradient, updated, new_mom = lax.map(one_replica, (tokens, cotangent, params, momentum))
    bit = jnp.remainder(step[0], 3).astype(jnp.int32)
    partner = jnp.bitwise_xor(jnp.arange(REPLICAS, dtype=jnp.int32), jnp.left_shift(jnp.int32(1), bit))
    averaged = 0.5 * (updated + jnp.take(updated, partner, axis=0))
    return (keys, input_gradient, averaged, new_mom)
```

```python
from functools import partial

import jax
import jax.numpy as jnp
from jax import lax
from jax.sharding import Mesh, PartitionSpec as P

BETA = 0.9
LRATE = 0.1
EPS = 1e-06
ROWS = ("z", "y")


def ring(n, by):
    return [(i, (i + by) % n) for i in range(n)]


def up(value):
    return lax.ppermute(value, "z", ring(lax.axis_size("z"), 1))


def down(value):
    return lax.ppermute(value, "z", ring(lax.axis_size("z"), -1))


def across(value):
    return lax.ppermute(value, "y", [(0, 1), (1, 0)])


def swapped(value, bit):
    mask = 2**bit
    pairs = [(source, source ^ mask) for source in range(lax.axis_size("rep"))]
    return lax.ppermute(value, "rep", pairs)


def after(value, *others):
    return lax.optimization_barrier((value,) + others)[0]


def wide(value):
    return value.astype(jnp.float32)


def narrow(value):
    return value.astype(jnp.bfloat16)


def exchange(own, make_parts, z, y):
    rows, width = own.shape
    half = rows // 2
    up1, down1, other = up(own), down(own), across(own)
    parts = make_parts().reshape(8, 2, rows, width)

    def part(by, column):
        return lax.dynamic_slice(
            parts, (jnp.remainder(z + by + 8, 8), column, 0, 0), (1, 1, rows, width)
        ).reshape(rows, width)

    def pair(by):
        return jnp.concatenate([part(by, 1 - y), part(-by, 1 - y)])

    up1, down1, other, far, third = lax.optimization_barrier(
        (up1, down1, other, part(4, 1 - y), pair(3))
    )
    up2 = up(jnp.concatenate([up1, other]))
    down2 = down(jnp.concatenate([other, down1]))
    far = across(far)
    third = across(third)

    sent = narrow(wide(part(4, y)) + wide(far))
    rising, falling = up(sent[:half]), down(sent[half:])
    rising = jnp.concatenate([rising, jnp.zeros((half, width), rising.dtype)])
    falling = jnp.concatenate([jnp.zeros((half, width), falling.dtype), falling])
    second = across(after(pair(2), far))

    up2, down2 = lax.optimization_barrier((up2, down2, sent))[:2]
    up3, down3 = up(up2), down(down2)

    def step(by, rising, falling, pair, *earlier):
        plus = wide(part(by, y)) + wide(pair[:rows]) + wide(rising)
        minus = wide(part(-by, y)) + wide(pair[rows:]) + wide(falling)
        plus, minus = lax.optimization_barrier((narrow(plus), narrow(minus)) + earlier)[:2]
        return up(plus), down(minus), plus

    rising, falling, sent = step(3, rising, falling, after(third, up2, down2))
    first = across(after(pair(1), third))

    up3, down3 = lax.optimization_barrier((up3, down3, sent))[:2]
    up4, down4 = up(up3[half:]), down(down3[: rows + half])

    rising, falling, sent = step(2, rising, falling, after(second, up3, down3))

    up4, down4 = lax.optimization_barrier((up4, down4, sent))[:2]
    far = jnp.concatenate([down4[rows:], up4[:half]])
    far_other = across(far)
    rising, falling, sent = step(1, rising, falling, after(first, up4, down4))
    here = across(after(part(0, 1 - y), first))

    whole = jnp.zeros((8, 2, rows, width), own.dtype)

    def put(whole, block, by, column):
        return lax.dynamic_update_slice(
            whole, block[None, None], (jnp.remainder(z + by + 8, 8), column, 0, 0)
        )

    for by, mine, others in (
        (0, own, other),
        (-1, up1, up2[rows:]),
        (1, down1, down2[:rows]),
        (-2, up2[:rows], up3[rows:]),
        (2, down2[rows:], down3[:rows]),
        (-3, up3[:rows], up4[half:]),
        (3, down3[rows:], down4[:rows]),
        (4, far, far_other),
    ):
        whole = put(whole, mine, by, y)
        whole = put(whole, others, by, 1 - y)

    def total():
        return wide(part(0, y)) + wide(here) + wide(rising) + wide(falling)

    return whole.reshape(16 * rows, width), sent, total


def local(tokens, gain, cotangent, params, momentum, step):
    width = tokens.shape[2]
    scale = width ** (-0.5)
    which = jnp.remainder(step[0], 3)
    z, y = lax.axis_index("z"), lax.axis_index("y")
    param_rows = params[0]
    input_rows = tokens[0].astype(jnp.float32)
    root_mean_square = jnp.sqrt(jnp.mean(input_rows * input_rows, axis=1, keepdims=True) + EPS)
    input_hat = input_rows / root_mean_square
    normalized_input = (input_hat * gain).astype(jnp.bfloat16)
    cot = cotangent[0]
    contract_last = (((1,), (1,)), ((), ()))
    contract_first = (((0,), (0,)), ((), ()))

    def make_parts():
        product = lax.dot_general(
            normalized_input, cot, contract_first, preferred_element_type=jnp.float32
        )
        return narrow(product * scale)

    whole, sent, total = exchange(narrow(param_rows), make_parts, z, y)
    key_sum = jnp.dot(normalized_input, after(whole, sent), preferred_element_type=jnp.float32)
    keys = narrow(key_sum * scale)

    new_mom = BETA * momentum[0] + total()
    updated = param_rows - LRATE * new_mom

    def finish(mine, whole, bit):
        peer = swapped(mine, bit)
        dnormed = lax.dot_general(cot, whole, contract_last, preferred_element_type=jnp.float32)
        incoming_gradient = dnormed * scale * gain
        inner_product = jnp.mean(incoming_gradient * input_hat, axis=1, keepdims=True)
        input_gradient = (incoming_gradient - input_hat * inner_product) / root_mean_square
        return peer, narrow(input_gradient)

    mine, whole = lax.optimization_barrier((narrow(updated), whole, keys))[:2]
    peer, input_gradient = lax.switch(
        which, [partial(finish, bit=b) for b in range(3)], mine, whole
    )
    averaged = 0.5 * (updated + wide(peer))
    return (keys[None], input_gradient[None], averaged[None], new_mom[None])


def solution(mesh):
    split = Mesh(mesh.devices.reshape(mesh.devices.shape[0], -1, 2), ("rep",) + ROWS)
    rows = P("rep", ROWS, None)
    return jax.shard_map(
        local,
        mesh=split,
        in_specs=(rows, P(), rows, rows, rows, P()),
        out_specs=(rows,) * 4,
        check_vma=False,
    )
```

```python
from functools import partial

import jax
import jax.numpy as jnp
from jax import lax
from jax.experimental import pallas as pl
from jax.experimental.pallas import tpu as pltpu
from jax.sharding import Mesh, PartitionSpec as P

BETA = 0.9
LRATE = 0.1
EPS = 1e-06
ROWS = ("z", "y")
FIRST = ((4, 1), (3, 1), (-3, 1), (4, 0))
SECOND = ((2, 1), (-2, 1), (1, 1), (-1, 1), (0, 1))
SECOND += ((3, 0), (-3, 0), (2, 0), (-2, 0), (1, 0), (-1, 0), (0, 0))


def ring(n, by):
    return [(i, (i + by) % n) for i in range(n)]


def up(value):
    return lax.ppermute(value, "z", ring(lax.axis_size("z"), 1))


def down(value):
    return lax.ppermute(value, "z", ring(lax.axis_size("z"), -1))


def across(value):
    return lax.ppermute(value, "y", [(0, 1), (1, 0)])


def swapped(value, bit):
    mask = 2**bit
    pairs = [(source, source ^ mask) for source in range(lax.axis_size("rep"))]
    return lax.ppermute(value, "rep", pairs)


def after(value, *others):
    return lax.optimization_barrier((value,) + others)[0]


def wide(value):
    return value.astype(jnp.float32)


def narrow(value):
    return value.astype(jnp.bfloat16)


def shard_at(by, column):
    z, y = lax.axis_index("z"), lax.axis_index("y")
    return 2 * lax.rem(z + (by + 8), 8) + lax.rem(y + column, 2)


def call(kernel, inputs, out_shape, scratch=(), anywhere=0, mib=44, flops=0, moved=0):
    vmem = pl.BlockSpec(memory_space=pltpu.VMEM)
    free = pl.BlockSpec(memory_space=pl.ANY)
    return pl.pallas_call(
        kernel,
        in_specs=[vmem] * (len(inputs) - anywhere) + [free] * anywhere,
        out_specs=[vmem] * len(out_shape),
        out_shape=[jax.ShapeDtypeStruct(shape, dtype) for shape, dtype in out_shape],
        scratch_shapes=list(scratch),
        compiler_params=pltpu.CompilerParams(vmem_limit_bytes=mib * 2**20),
        cost_estimate=pl.CostEstimate(flops=flops, bytes_accessed=moved, transcendentals=0),
    )(*inputs)


def cast_kernel(params, out):
    out[...] = params[...].astype(out.dtype)


def gain_row(gain):
    return jnp.concatenate([gain[i : i + 1, :] for i in range(gain.shape[0])], axis=1)


def grad_part(block, cot, out, at):
    part, features = block.shape[1], cot.shape[1]
    scale = (16 * part) ** (-0.5)
    for col in range(0, features, 256):
        product = lax.dot_general(
            block,
            cot[:, col : col + 256],
            (((0,), (0,)), ((), ())),
            preferred_element_type=jnp.float32,
        )
        out[at : at + part, col : col + 256] = (product * scale).astype(out.dtype)


def first_kernel(tokens, gain, cot, blocks, inverse, early, far_own):
    count, rows, part = blocks.shape
    width = tokens.shape[1]
    chunk = 64
    gains = gain_row(gain)

    @pl.loop(0, rows // chunk)
    def _(i):
        here = pl.ds(pl.multiple_of(i * chunk, chunk), chunk)
        x = tokens[here, :].astype(jnp.float32)
        inv = lax.rsqrt(jnp.sum(x * x, axis=1, keepdims=True) * (1.0 / width) + EPS)
        inverse[here, :] = inv
        normalized = ((x * inv) * gains).astype(jnp.bfloat16)
        for j in range(count):
            blocks[j, here, :] = normalized[:, j * part : (j + 1) * part]

    places = ((early, 0), (early, part), (early, 2 * part), (far_own, 0))
    for (by, column), (out, at) in zip(FIRST, places):
        grad_part(blocks[shard_at(by, column)], cot, out, at)


def second_kernel(blocks, cot, *outs):
    part = blocks.shape[2]
    places = [(out, at) for out in outs for at in range(0, out.shape[0], part)]
    for (by, column), (out, at) in zip(SECOND, places):
        grad_part(blocks[shard_at(by, column)], cot, out, at)


def pieces(part):
    half = part // 2
    return (
        (0, 0, part, 0, 0, 0),
        (1, 0, part, 0, 1, 0),
        (2, 0, part, -1, 0, 0),
        (3, 0, part, 1, 0, 0),
        (4, 0, part, -2, 0, 0),
        (4, part, part, -1, 1, 0),
        (5, 0, part, 1, 1, 0),
        (5, part, part, 2, 0, 0),
        (6, 0, part, -3, 0, 0),
        (6, part, part, -2, 1, 0),
        (7, 0, part, 2, 1, 0),
        (7, part, part, 3, 0, 0),
        (8, 0, half, 4, 0, half),
        (8, half, part, -3, 1, 0),
        (9, 0, part, 3, 1, 0),
        (9, part, half, 4, 0, 0),
        (10, 0, part, 4, 1, 0),
    )


def load_rows(gathered, whole, sems, part):
    copies = []
    for i, (array, at, count, by, column, inner) in enumerate(pieces(part)):
        to = pl.multiple_of(shard_at(by, column) * part + inner, 16)
        copies.append(
            pltpu.make_async_copy(
                gathered[array].at[pl.ds(at, count), :], whole.at[pl.ds(to, count), :], sems.at[i]
            )
        )
    for copy in copies:
        copy.start()
    return copies


def keys_kernel(tokens, gain, inverse, *rest):
    gathered, (keys, whole, normalized, sems) = rest[:11], rest[11:]
    rows, width = tokens.shape
    copies = load_rows(gathered, whole, sems, width // 16)
    chunk = 64
    gains = gain_row(gain)

    @pl.loop(0, rows // chunk)
    def _(i):
        here = pl.ds(pl.multiple_of(i * chunk, chunk), chunk)
        x = tokens[here, :].astype(jnp.float32)
        normalized[here, :] = ((x * inverse[here, :]) * gains).astype(jnp.bfloat16)

    for copy in copies:
        copy.wait()
    for col in range(0, keys.shape[1], 256):
        product = jnp.dot(
            normalized[...], whole[:, col : col + 256], preferred_element_type=jnp.float32
        )
        keys[:, col : col + 256] = (product * width ** (-0.5)).astype(keys.dtype)


def input_kernel(tokens, gain, inverse, cot, *rest):
    gathered, (out, whole, upstream, sems) = rest[:11], rest[11:]
    rows, width = tokens.shape
    copies = load_rows(gathered, whole, sems, width // 16)
    gains = gain_row(gain) * width ** (-0.5)
    inv = inverse[...]
    for copy in copies:
        copy.wait()
    total = jnp.zeros((rows, 1), jnp.float32)
    cols = 256
    for col in range(0, width, cols):
        product = lax.dot_general(
            cot[...],
            whole[col : col + cols, :],
            (((1,), (1,)), ((), ())),
            preferred_element_type=jnp.float32,
        )
        value = product * gains[:, col : col + cols]
        upstream[:, col : col + cols] = value
        total += jnp.sum(
            value * tokens[:, col : col + cols].astype(jnp.float32), axis=1, keepdims=True
        )
    inverse_total = total * inv * inv * (1.0 / width)
    chunk = 64
    upstream_scale = inv
    token_scale = inverse_total * inv
    for at in range(0, rows, chunk):
        x = tokens[at : at + chunk, :].astype(jnp.float32)
        value = upstream[at : at + chunk, :] * upstream_scale[at : at + chunk]
        out[at : at + chunk, :] = (value - x * token_scale[at : at + chunk]).astype(out.dtype)


def local(tokens, gain, cotangent, params, momentum, step):
    rows, width = tokens.shape[1:]
    features = cotangent.shape[2]
    part, half = params.shape[1], params.shape[1] // 2
    which = jnp.remainder(step[0], 3)
    param_rows, tokens, cot = params[0], tokens[0], cotangent[0]
    gain = gain.reshape(width // 128, 128)
    bf16, f32 = jnp.bfloat16, jnp.float32

    def sums(*counts):
        return [((n * part, features), bf16) for n in counts]

    product = 2 * rows * part * features
    (own,) = call(cast_kernel, [param_rows], sums(1), moved=2**20)
    up1, down1, other = up(own), down(own), across(own)
    blocks, inverse, early, far_own = call(
        first_kernel,
        [tokens, gain, cot],
        [((16, rows, part), bf16), ((rows, 1), f32)] + sums(3, 1),
        flops=4 * product,
        moved=11 * 2**20,
    )
    up2, down2 = jnp.concatenate([up1, other]), jnp.concatenate([other, down1])
    up2, down2, blocks = lax.optimization_barrier((up2, down2, blocks))
    up2, down2 = up(up2), down(down2)
    early = across(early)
    late, here, own3, own2, own1, own0 = call(
        second_kernel, [blocks, cot], sums(4, 1, 2, 2, 2, 1), flops=12 * product, moved=11 * 2**20
    )
    late = across(late)

    up3, down3 = up(up2), down(down2)

    def reduced(owns, received, rising, falling, *earlier):
        plus = wide(owns[:part]) + wide(received[:part]) + wide(rising)
        minus = wide(owns[part:]) + wide(received[part:]) + wide(falling)
        return lax.optimization_barrier((narrow(plus), narrow(minus)) + earlier)[:2]

    sent = narrow(wide(far_own) + wide(early[:part]))
    rising, falling = up(sent[:half]), down(sent[half:])
    rising = jnp.concatenate([rising, jnp.zeros((half, features), bf16)])
    falling = jnp.concatenate([jnp.zeros((half, features), bf16), falling])
    plus, minus = reduced(own3, early[part:], rising, falling, up2, down2)
    rising, falling = up(plus), down(minus)

    up4, down4 = up(up3[half:]), down(down3[: part + half])
    plus, minus = reduced(own2, late[: 2 * part], rising, falling, up3, down3)
    rising, falling = up(plus), down(minus)
    far = jnp.concatenate([down4[part:], up4[:half]])
    far_other = across(far)
    here = across(after(here, far))
    plus, minus = reduced(own1, late[2 * part :], rising, falling, up4, down4)
    rising, falling = up(plus), down(minus)

    gathered = [own, other, up1, down1, up2, down2, up3, down3, up4, down4, far_other]
    scratch = [pltpu.VMEM((width, features), bf16)]
    sems = [pltpu.SemaphoreType.DMA((17,))]
    (keys,) = call(
        keys_kernel,
        [after(tokens, plus, minus), gain, inverse] + gathered,
        [((rows, features), bf16)],
        scratch + [pltpu.VMEM((rows, width), bf16)] + sems,
        11,
        flops=16 * product,
        moved=13 * 2**20,
    )
    new_mom = BETA * momentum[0] + (wide(own0) + wide(here) + wide(rising) + wide(falling))
    updated = param_rows - LRATE * new_mom

    def finish(mine, tokens, cot, gain, inverse, *gathered, bit):
        peer = swapped(mine, bit)
        (input_gradient,) = call(
            input_kernel,
            [tokens, gain, inverse, cot, *gathered],
            [((rows, width), bf16)],
            scratch + [pltpu.VMEM((rows, width), f32)] + sems,
            11,
            flops=16 * product,
            moved=16 * 2**20,
        )
        return peer, input_gradient

    mine = after(narrow(updated), keys)
    peer, input_gradient = lax.switch(
        which,
        [partial(finish, bit=b) for b in range(3)],
        *(mine, tokens, cot, gain, inverse, *gathered),
    )
    averaged = 0.5 * (updated + wide(peer))
    return (keys[None], input_gradient[None], averaged[None], new_mom[None])


def solution(mesh):
    split = Mesh(mesh.devices.reshape(mesh.devices.shape[0], -1, 2), ("rep",) + ROWS)
    rows = P("rep", ROWS, None)
    return jax.shard_map(
        local,
        mesh=split,
        in_specs=(rows, P(), rows, rows, rows, P()),
        out_specs=(rows,) * 4,
        check_vma=False,
    )
```

```python
from functools import partial

import jax
import jax.numpy as jnp
from jax import lax
from jax.experimental import pallas as pl
from jax.experimental.pallas import tpu as pltpu
from jax.sharding import Mesh, PartitionSpec as P

BETA = 0.9
LRATE = 0.1
EPS = 1e-06
ROWS = ("z", "y")
FIRST = ((4, 1), (3, 1), (-3, 1), (4, 0))
SECOND = ((2, 1), (-2, 1), (1, 1), (-1, 1), (0, 1))
SECOND += ((3, 0), (-3, 0), (2, 0), (-2, 0), (1, 0), (-1, 0), (0, 0))


def ring(n, by):
    return [(i, (i + by) % n) for i in range(n)]


def up(value):
    return lax.ppermute(value, "z", ring(lax.axis_size("z"), 1))


def down(value):
    return lax.ppermute(value, "z", ring(lax.axis_size("z"), -1))


def across(value):
    return lax.ppermute(value, "y", [(0, 1), (1, 0)])


def swapped(value, bit):
    mask = 2**bit
    pairs = [(source, source ^ mask) for source in range(lax.axis_size("rep"))]
    return lax.ppermute(value, "rep", pairs)


def after(value, *others):
    return lax.optimization_barrier((value,) + others)[0]


def wide(value):
    return value.astype(jnp.float32)


def narrow(value):
    return value.astype(jnp.bfloat16)


def shard_at(by, column):
    z, y = lax.axis_index("z"), lax.axis_index("y")
    return 2 * lax.rem(z + (by + 8), 8) + lax.rem(y + column, 2)


def call(kernel, inputs, out_shape, scratch=(), anywhere=0, mib=32, flops=0, moved=0, aliases=None):
    vmem = pl.BlockSpec(memory_space=pltpu.VMEM)
    free = pl.BlockSpec(memory_space=pl.ANY)
    return pl.pallas_call(
        kernel,
        in_specs=[vmem] * (len(inputs) - anywhere) + [free] * anywhere,
        out_specs=[vmem] * len(out_shape),
        out_shape=[jax.ShapeDtypeStruct(shape, dtype) for shape, dtype in out_shape],
        scratch_shapes=list(scratch),
        input_output_aliases=aliases or {},
        compiler_params=pltpu.CompilerParams(vmem_limit_bytes=mib * 2**20),
        cost_estimate=pl.CostEstimate(flops=flops, bytes_accessed=moved, transcendentals=0),
    )(*inputs)


def cast_kernel(params, out):
    out[...] = params[...].astype(out.dtype)


def gain_row(gain):
    return jnp.concatenate([gain[i : i + 1, :] for i in range(gain.shape[0])], axis=1)


def grad_part(block, cot, out, at):
    part, features = block.shape[1], cot.shape[1]
    scale = (16 * part) ** (-0.5)
    for col in range(0, features, 256):
        product = lax.dot_general(
            block,
            cot[:, col : col + 256],
            (((0,), (0,)), ((), ())),
            preferred_element_type=jnp.float32,
        )
        out[at : at + part, col : col + 256] = (product * scale).astype(out.dtype)


def first_kernel(tokens, gain, cot, blocks, whole, inverse, far, third, far_own):
    count, rows, part = blocks.shape
    width = tokens.shape[1]
    chunk = 64
    gains = gain_row(gain)

    @pl.loop(0, rows // chunk)
    def _(i):
        here = pl.ds(pl.multiple_of(i * chunk, chunk), chunk)
        x = tokens[here, :].astype(jnp.float32)
        inv = lax.rsqrt(jnp.sum(x * x, axis=1, keepdims=True) * (1.0 / width) + EPS)
        inverse[here, :] = inv
        normalized = ((x * inv) * gains).astype(jnp.bfloat16)
        whole[here, :] = normalized
        for j in range(count):
            blocks[j, here, :] = normalized[:, j * part : (j + 1) * part]

    places = ((far, 0), (third, 0), (third, part), (far_own, 0))
    for (by, column), (out, at) in zip(FIRST, places):
        grad_part(blocks[shard_at(by, column)], cot, out, at)


def second_kernel(blocks, cot, *outs):
    part = blocks.shape[2]
    places = [(out, at) for out in outs for at in range(0, out.shape[0], part)]
    for (by, column), (out, at) in zip(SECOND, places):
        grad_part(blocks[shard_at(by, column)], cot, out, at)


def pieces(part):
    half = part // 2
    return (
        (0, 0, part, 0, 0, 0),
        (1, 0, part, 0, 1, 0),
        (2, 0, part, -1, 0, 0),
        (3, 0, part, 1, 0, 0),
        (4, 0, part, -2, 0, 0),
        (4, part, part, -1, 1, 0),
        (5, 0, part, 1, 1, 0),
        (5, part, part, 2, 0, 0),
        (6, 0, part, -3, 0, 0),
        (6, part, part, -2, 1, 0),
        (7, 0, part, 2, 1, 0),
        (7, part, part, 3, 0, 0),
        (8, 0, half, 4, 0, half),
        (8, half, part, -3, 1, 0),
        (9, 0, part, 3, 1, 0),
        (9, part, half, 4, 0, 0),
        (10, 0, part, 4, 1, 0),
    )


def load_rows(wanted, gathered, whole, sems):
    part = whole.shape[0] // 16
    copies = []
    for i, (array, at, count, by, column, inner) in enumerate(wanted):
        to = pl.multiple_of(shard_at(by, column) * part + inner, 16)
        copies.append(
            pltpu.make_async_copy(
                gathered[array].at[pl.ds(at, count), :], whole.at[pl.ds(to, count), :], sems.at[i]
            )
        )
    for copy in copies:
        copy.start()
    for copy in copies:
        copy.wait()


def near_kernel(*refs):
    gathered, (whole, sems) = refs[:8], refs[8:]
    wanted = [piece for piece in pieces(whole.shape[0] // 16) if piece[0] < 8]
    load_rows(wanted, gathered, whole, sems)


def keys_kernel(normalized, near, *refs):
    gathered, (keys, whole, sems) = refs[:3], refs[3:]
    width = whole.shape[0]
    wanted = [piece for piece in pieces(width // 16) if piece[0] >= 8]
    whole[...] = near[...]
    load_rows(wanted, (None,) * 8 + tuple(gathered), whole, sems)
    for col in range(0, keys.shape[1], 256):
        product = jnp.dot(
            normalized[...], whole[:, col : col + 256], preferred_element_type=jnp.float32
        )
        keys[:, col : col + 256] = (product * width ** (-0.5)).astype(keys.dtype)


def input_kernel(tokens, gain, inverse, cot, whole, out, upstream):
    rows, width = tokens.shape
    gains = gain_row(gain) * width ** (-0.5)
    inv = inverse[...]
    total = jnp.zeros((rows, 1), jnp.float32)
    cols = 256
    for col in range(0, width, cols):
        product = lax.dot_general(
            cot[...],
            whole[col : col + cols, :],
            (((1,), (1,)), ((), ())),
            preferred_element_type=jnp.float32,
        )
        value = product * gains[:, col : col + cols]
        upstream[:, col : col + cols] = value
        total += jnp.sum(
            value * tokens[:, col : col + cols].astype(jnp.float32), axis=1, keepdims=True
        )
    token_scale = total * inv * inv * inv * (1.0 / width)
    chunk = 64
    for at in range(0, rows, chunk):
        here = slice(at, at + chunk)
        x = tokens[here, :].astype(jnp.float32)
        out[here, :] = (upstream[here, :] * inv[here] - x * token_scale[here]).astype(out.dtype)


def update_kernel(own, here, rising, falling, params, momentum, new_momentum, updated, sent):
    grad = own[...].astype(jnp.float32) + here[...].astype(jnp.float32)
    grad += rising[...].astype(jnp.float32) + falling[...].astype(jnp.float32)
    moved = BETA * momentum[...] + grad
    new_momentum[...] = moved
    value = params[...] - LRATE * moved
    updated[...] = value
    sent[...] = value.astype(sent.dtype)


def average_kernel(updated, peer, out):
    out[...] = 0.5 * (updated[...] + peer[...].astype(jnp.float32))


def local(tokens, gain, cotangent, params, momentum, step):
    rows, width = tokens.shape[1:]
    features = cotangent.shape[2]
    part, half = params.shape[1], params.shape[1] // 2
    which = jnp.remainder(step[0], 3)
    param_rows, tokens, cot = params[0], tokens[0], cotangent[0]
    gain = gain.reshape(width // 128, 128)
    bf16, f32 = jnp.bfloat16, jnp.float32

    def sums(*counts):
        return [((n * part, features), bf16) for n in counts]

    product = 2 * rows * part * features
    (own,) = call(cast_kernel, [param_rows], sums(1), moved=2**20)
    up1, down1, other = up(own), down(own), across(own)
    blocks, normalized, inverse, far, third, far_own = call(
        first_kernel,
        [tokens, gain, cot],
        [((16, rows, part), bf16), ((rows, width), bf16), ((rows, 1), f32)] + sums(1, 2, 1),
        flops=4 * product,
        moved=11 * 2**20,
    )
    up2, down2 = jnp.concatenate([up1, other]), jnp.concatenate([other, down1])
    far = across(far)
    up2, down2, third, blocks = lax.optimization_barrier((up2, down2, third, blocks))
    up2, down2, third = up(up2), down(down2), across(third)
    second, first, here, own3, own2, own1, own0 = call(
        second_kernel,
        [blocks, cot],
        sums(2, 2, 1, 2, 2, 2, 1),
        flops=12 * product,
        moved=11 * 2**20,
    )

    def reduced(owns, received, rising, falling, *earlier):
        plus = wide(owns[:part]) + wide(received[:part]) + wide(rising)
        minus = wide(owns[part:]) + wide(received[part:]) + wide(falling)
        return lax.optimization_barrier((narrow(plus), narrow(minus)) + earlier)[:2]

    sent = narrow(wide(far_own) + wide(far))
    rising, falling = up(sent[:half]), down(sent[half:])
    up2, down2, rising, falling = lax.optimization_barrier((up2, down2, rising, falling))
    up3, down3 = up(up2), down(down2)
    second = across(after(second, up2, down2))
    rising = jnp.concatenate([rising, jnp.zeros((half, features), bf16)])
    falling = jnp.concatenate([jnp.zeros((half, features), bf16), falling])
    plus, minus = reduced(own3, third, rising, falling, up2, down2)
    rising, falling = up(plus), down(minus)

    up4, down4 = up(up3[half:]), down(down3[: part + half])
    first = across(after(first, up3, down3))
    near = [own, other, up1, down1, up2, down2, up3, down3]
    (weight,) = call(
        near_kernel,
        [after(own, plus, minus)] + near[1:],
        sums(16),
        [pltpu.SemaphoreType.DMA((12,))],
        8,
        moved=11 * 2**20,
    )
    plus, minus = reduced(own2, second, rising, falling, up3, down3, weight)
    rising, falling = up(plus), down(minus)
    far_rows = jnp.concatenate([down4[part:], up4[:half]])
    far_other = across(far_rows)
    here = across(after(here, far_rows))
    plus, minus = reduced(own1, first, rising, falling, up4, down4)
    rising, falling = up(plus), down(minus)

    keys, weight = call(
        keys_kernel,
        [normalized, after(weight, plus, minus), up4, down4, far_other],
        [((rows, features), bf16)] + sums(16),
        [pltpu.SemaphoreType.DMA((5,))],
        3,
        flops=16 * product,
        moved=13 * 2**20,
        aliases={1: 1},
    )
    stored = ((part, features), f32)
    new_momentum, updated, sent = call(
        update_kernel,
        [own0, here, rising, falling, param_rows, momentum[0]],
        [stored, stored] + sums(1),
        moved=6 * 2**20,
    )

    def finish(sent, tokens, cot, gain, inverse, weight, bit):
        peer = swapped(sent, bit)
        (input_gradient,) = call(
            input_kernel,
            [tokens, gain, inverse, cot, weight],
            [((rows, width), bf16)],
            [pltpu.VMEM((rows, width), f32)],
            flops=16 * product,
            moved=16 * 2**20,
        )
        return peer, input_gradient

    peer, input_gradient = lax.switch(
        which,
        [partial(finish, bit=b) for b in range(3)],
        *(after(sent, keys), tokens, cot, gain, inverse, weight),
    )
    (averaged,) = call(average_kernel, [updated, peer], [stored], moved=2 * 2**20)
    return (keys[None], input_gradient[None], averaged[None], new_momentum[None])


def solution(mesh):
    split = Mesh(mesh.devices.reshape(mesh.devices.shape[0], -1, 2), ("rep",) + ROWS)
    rows = P("rep", ROWS, None)
    return jax.shard_map(
        local,
        mesh=split,
        in_specs=(rows, P(), rows, rows, rows, P()),
        out_specs=(rows,) * 4,
        check_vma=False,
    )
```

```python
from functools import partial

import jax
import jax.numpy as jnp
from jax import lax
from jax.experimental import pallas as pl
from jax.experimental.pallas import tpu as pltpu
from jax.sharding import Mesh, PartitionSpec as P

BETA = 0.9
LRATE = 0.1
EPS = 1e-06
ROWS = ("z", "y")
FIRST = ((4, 1), (3, 1), (-3, 1), (4, 0))
SECOND = ((2, 1), (-2, 1), (1, 1), (-1, 1), (0, 1))
SECOND += ((3, 0), (-3, 0), (2, 0), (-2, 0), (1, 0), (-1, 0), (0, 0))


def ring(n, by):
    return [(i, (i + by) % n) for i in range(n)]


def up(value):
    return lax.ppermute(value, "z", ring(lax.axis_size("z"), 1))


def down(value):
    return lax.ppermute(value, "z", ring(lax.axis_size("z"), -1))


def across(value):
    return lax.ppermute(value, "y", [(0, 1), (1, 0)])


def swapped(value, bit):
    mask = 2**bit
    pairs = [(source, source ^ mask) for source in range(lax.axis_size("rep"))]
    return lax.ppermute(value, "rep", pairs)


def after(value, *others):
    return lax.optimization_barrier((value,) + others)[0]


def wide(value):
    return value.astype(jnp.float32)


def narrow(value):
    return value.astype(jnp.bfloat16)


def shard_at(by, column):
    z, y = lax.axis_index("z"), lax.axis_index("y")
    return 2 * lax.rem(z + (by + 8), 8) + lax.rem(y + column, 2)


def call(kernel, inputs, out_shape, scratch=(), anywhere=0, mib=16, flops=0, moved=0):
    vmem = pl.BlockSpec(memory_space=pltpu.VMEM)
    free = pl.BlockSpec(memory_space=pl.ANY)
    return pl.pallas_call(
        kernel,
        in_specs=[vmem] * (len(inputs) - anywhere) + [free] * anywhere,
        out_specs=[vmem] * len(out_shape),
        out_shape=[jax.ShapeDtypeStruct(shape, dtype) for shape, dtype in out_shape],
        scratch_shapes=list(scratch),
        compiler_params=pltpu.CompilerParams(vmem_limit_bytes=mib * 2**20),
        cost_estimate=pl.CostEstimate(flops=flops, bytes_accessed=moved, transcendentals=0),
    )(*inputs)


def cast_kernel(params, out):
    out[...] = params[...].astype(out.dtype)


def gain_row(gain):
    return jnp.concatenate([gain[i : i + 1, :] for i in range(gain.shape[0])], axis=1)


def grad_part(block, cot, out, at):
    part, features = block.shape[1], cot.shape[1]
    scale = (16 * part) ** (-0.5)
    for col in range(0, features, 256):
        product = lax.dot_general(
            block,
            cot[:, col : col + 256],
            (((0,), (0,)), ((), ())),
            preferred_element_type=jnp.float32,
        )
        out[at : at + part, col : col + 256] = (product * scale).astype(out.dtype)


def first_kernel(tokens, gain, cot, blocks, whole, inverse, far, third, far_own):
    count, rows, part = blocks.shape
    width = tokens.shape[1]
    chunk = 64
    gains = gain_row(gain)

    @pl.loop(0, rows // chunk)
    def _(i):
        here = pl.ds(pl.multiple_of(i * chunk, chunk), chunk)
        x = tokens[here, :].astype(jnp.float32)
        inv = lax.rsqrt(jnp.sum(x * x, axis=1, keepdims=True) * (1.0 / width) + EPS)
        inverse[here, :] = inv
        normalized = ((x * inv) * gains).astype(jnp.bfloat16)
        whole[here, :] = normalized
        for j in range(count):
            blocks[j, here, :] = normalized[:, j * part : (j + 1) * part]

    places = ((far, 0), (third, 0), (third, part), (far_own, 0))
    for (by, column), (out, at) in zip(FIRST, places):
        grad_part(blocks[shard_at(by, column)], cot, out, at)


def second_kernel(blocks, cot, *outs):
    part = blocks.shape[2]
    places = [(out, at) for out in outs for at in range(0, out.shape[0], part)]
    for (by, column), (out, at) in zip(SECOND, places):
        grad_part(blocks[shard_at(by, column)], cot, out, at)


def pieces(part):
    half = part // 2
    return (
        (0, 0, part, 0, 0, 0),
        (1, 0, part, 0, 1, 0),
        (2, 0, part, -1, 0, 0),
        (3, 0, part, 1, 0, 0),
        (4, 0, part, -2, 0, 0),
        (4, part, part, -1, 1, 0),
        (5, 0, part, 1, 1, 0),
        (5, part, part, 2, 0, 0),
        (6, 0, part, -3, 0, 0),
        (6, part, part, -2, 1, 0),
        (7, 0, part, 2, 1, 0),
        (7, part, part, 3, 0, 0),
        (8, 0, half, 4, 0, half),
        (8, half, part, -3, 1, 0),
        (9, 0, part, 3, 1, 0),
        (9, part, half, 4, 0, 0),
        (10, 0, part, 4, 1, 0),
    )


def lay_out(gathered, whole):
    part = whole.shape[0] // 16
    for array, at, count, by, column, inner in pieces(part):
        to = pl.multiple_of(shard_at(by, column) * part + inner, 16)
        whole[pl.ds(to, count), :] = gathered[array][at : at + count, :]


def keys_kernel(normalized, *refs):
    gathered, (keys, whole) = refs[:11], refs[11:]
    lay_out(gathered, whole)
    for col in range(0, keys.shape[1], 256):
        product = jnp.dot(
            normalized[...], whole[:, col : col + 256], preferred_element_type=jnp.float32
        )
        keys[:, col : col + 256] = (product * whole.shape[0] ** (-0.5)).astype(keys.dtype)


def input_kernel(gain, inverse, cot, *refs):
    gathered, (source, out, tokens, whole, upstream, sem) = refs[:11], refs[11:]
    rows, width = tokens.shape
    copy = pltpu.make_async_copy(source, tokens, sem)
    copy.start()
    lay_out(gathered, whole)
    copy.wait()
    gains = gain_row(gain) * width ** (-0.5)
    inv = inverse[...]
    total = jnp.zeros((rows, 1), jnp.float32)
    cols = 256
    for col in range(0, width, cols):
        product = lax.dot_general(
            cot[...],
            whole[col : col + cols, :],
            (((1,), (1,)), ((), ())),
            preferred_element_type=jnp.float32,
        )
        value = product * gains[:, col : col + cols]
        upstream[:, col : col + cols] = value
        total += jnp.sum(
            value * tokens[:, col : col + cols].astype(jnp.float32), axis=1, keepdims=True
        )
    token_scale = total * inv * inv * inv * (1.0 / width)
    chunk = 64
    for at in range(0, rows, chunk):
        here = slice(at, at + chunk)
        x = tokens[here, :].astype(jnp.float32)
        out[here, :] = (upstream[here, :] * inv[here] - x * token_scale[here]).astype(out.dtype)


def update_kernel(own, here, rising, falling, params, momentum, new_momentum, updated, sent):
    grad = own[...].astype(jnp.float32) + here[...].astype(jnp.float32)
    grad += rising[...].astype(jnp.float32) + falling[...].astype(jnp.float32)
    moved = BETA * momentum[...] + grad
    new_momentum[...] = moved
    value = params[...] - LRATE * moved
    updated[...] = value
    sent[...] = value.astype(sent.dtype)


def average_kernel(updated, peer, out):
    out[...] = 0.5 * (updated[...] + peer[...].astype(jnp.float32))


def local(tokens, gain, cotangent, params, momentum, step):
    rows, width = tokens.shape[1:]
    features = cotangent.shape[2]
    part, half = params.shape[1], params.shape[1] // 2
    which = jnp.remainder(step[0], 3)
    param_rows, tokens, cot = params[0], tokens[0], cotangent[0]
    gain = gain.reshape(width // 128, 128)
    bf16, f32 = jnp.bfloat16, jnp.float32

    def sums(*counts):
        return [((n * part, features), bf16) for n in counts]

    product = 2 * rows * part * features
    (own,) = call(cast_kernel, [param_rows], sums(1), moved=2**20)
    up1, down1, other = up(own), down(own), across(own)
    blocks, normalized, inverse, far, third, far_own = call(
        first_kernel,
        [tokens, gain, cot],
        [((16, rows, part), bf16), ((rows, width), bf16), ((rows, 1), f32)] + sums(1, 2, 1),
        flops=4 * product,
        moved=11 * 2**20,
    )
    up2, down2 = jnp.concatenate([up1, other]), jnp.concatenate([other, down1])
    far = across(far)
    up2, down2, third, blocks = lax.optimization_barrier((up2, down2, third, blocks))
    up2, down2, third = up(up2), down(down2), across(third)
    second, first, here, own3, own2, own1, own0 = call(
        second_kernel,
        [blocks, cot],
        sums(2, 2, 1, 2, 2, 2, 1),
        flops=12 * product,
        moved=11 * 2**20,
    )

    def reduced(owns, received, rising, falling, *earlier):
        plus = wide(owns[:part]) + wide(received[:part]) + wide(rising)
        minus = wide(owns[part:]) + wide(received[part:]) + wide(falling)
        return lax.optimization_barrier((narrow(plus), narrow(minus)) + earlier)[:2]

    sent = narrow(wide(far_own) + wide(far))
    up3 = up(jnp.concatenate([up2, sent[:half]]))
    down3 = down(jnp.concatenate([down2, sent[half:]]))
    second = across(after(second, third))
    empty = jnp.zeros((half, features), bf16)
    rising = jnp.concatenate([up3[2 * part :], empty])
    falling = jnp.concatenate([empty, down3[2 * part :]])
    plus, minus = reduced(own3, third, rising, falling)
    rising, falling = up(plus), down(minus)

    up4, down4 = up(up3[half : 2 * part]), down(down3[: part + half])
    first = across(after(first, second))
    plus, minus = reduced(own2, second, rising, falling, up3, down3)
    rising, falling = up(plus), down(minus)
    far_rows = jnp.concatenate([down4[part:], up4[:half]])
    far_other = across(far_rows)
    here = across(after(here, far_rows))
    plus, minus = reduced(own1, first, rising, falling, up4, down4)
    rising, falling = up(plus), down(minus)

    gathered = [own, other, up1, down1, up2, down2, up3, down3, up4, down4, far_other]
    whole = pltpu.VMEM((width, features), bf16)
    (keys,) = call(
        keys_kernel,
        [after(normalized, plus, minus)] + gathered,
        [((rows, features), bf16)],
        [whole],
        mib=24,
        flops=16 * product,
        moved=13 * 2**20,
    )
    stored = ((part, features), f32)
    new_momentum, updated, sent = call(
        update_kernel,
        [own0, here, rising, falling, param_rows, momentum[0]],
        [stored, stored] + sums(1),
        moved=6 * 2**20,
    )

    def finish(sent, gain, inverse, cot, *others, bit):
        peer = swapped(sent, bit)
        (input_gradient,) = call(
            input_kernel,
            [gain, inverse, cot, *others],
            [((rows, width), bf16)],
            [
                pltpu.VMEM((rows, width), bf16),
                whole,
                pltpu.VMEM((rows, width), f32),
                pltpu.SemaphoreType.DMA,
            ],
            1,
            mib=36,
            flops=16 * product,
            moved=16 * 2**20,
        )
        return peer, input_gradient

    peer, input_gradient = lax.switch(
        which,
        [partial(finish, bit=b) for b in range(3)],
        *(after(sent, keys), gain, inverse, cot, *gathered, tokens),
    )
    (averaged,) = call(average_kernel, [updated, peer], [stored], moved=2 * 2**20)
    return (keys[None], input_gradient[None], averaged[None], new_momentum[None])


def solution(mesh):
    split = Mesh(mesh.devices.reshape(mesh.devices.shape[0], -1, 2), ("rep",) + ROWS)
    rows = P("rep", ROWS, None)
    return jax.shard_map(
        local,
        mesh=split,
        in_specs=(rows, P(), rows, rows, rows, P()),
        out_specs=(rows,) * 4,
        check_vma=False,
    )
```

```python
from functools import partial

import jax
import jax.numpy as jnp
from jax import lax
from jax.experimental import pallas as pl
from jax.experimental.pallas import tpu as pltpu
from jax.sharding import Mesh, PartitionSpec as P

BETA = 0.9
LRATE = 0.1
EPS = 1e-06
ROWS = ("z", "y")
FIRST = ((4, 1), (3, 1), (-3, 1), (4, 0))
SECOND = ((2, 1), (-2, 1), (1, 1), (-1, 1), (0, 1))
SECOND += ((3, 0), (-3, 0), (2, 0), (-2, 0), (1, 0), (-1, 0), (0, 0))


def ring(n, by):
    return [(i, (i + by) % n) for i in range(n)]


def up(value):
    return lax.ppermute(value, "z", ring(lax.axis_size("z"), 1))


def down(value):
    return lax.ppermute(value, "z", ring(lax.axis_size("z"), -1))


def across(value):
    return lax.ppermute(value, "y", [(0, 1), (1, 0)])


def swapped(value, bit):
    mask = 2**bit
    pairs = [(source, source ^ mask) for source in range(lax.axis_size("rep"))]
    return lax.ppermute(value, "rep", pairs)


def after(value, *others):
    return lax.optimization_barrier((value,) + others)[0]


def wide(value):
    return value.astype(jnp.float32)


def narrow(value):
    return value.astype(jnp.bfloat16)


def shard_at(by, column):
    z, y = lax.axis_index("z"), lax.axis_index("y")
    return 2 * lax.rem(z + (by + 8), 8) + lax.rem(y + column, 2)


def call(kernel, inputs, out_shape, scratch=(), anywhere=0, mib=16, flops=0, moved=0):
    vmem = pl.BlockSpec(memory_space=pltpu.VMEM)
    free = pl.BlockSpec(memory_space=pl.ANY)
    return pl.pallas_call(
        kernel,
        in_specs=[vmem] * (len(inputs) - anywhere) + [free] * anywhere,
        out_specs=[vmem] * len(out_shape),
        out_shape=[jax.ShapeDtypeStruct(shape, dtype) for shape, dtype in out_shape],
        scratch_shapes=list(scratch),
        compiler_params=pltpu.CompilerParams(vmem_limit_bytes=mib * 2**20),
        cost_estimate=pl.CostEstimate(flops=flops, bytes_accessed=moved, transcendentals=0),
    )(*inputs)


def cast_kernel(params, out):
    out[...] = params[...].astype(out.dtype)


def gain_row(gain):
    return jnp.concatenate([gain[i : i + 1, :] for i in range(gain.shape[0])], axis=1)


def grad_part(block, cot, out, at):
    part, features = block.shape[1], cot.shape[1]
    scale = (16 * part) ** (-0.5)
    for col in range(0, features, 256):
        product = lax.dot_general(
            block,
            cot[:, col : col + 256],
            (((0,), (0,)), ((), ())),
            preferred_element_type=jnp.float32,
        )
        out[at : at + part, col : col + 256] = (product * scale).astype(out.dtype)


def first_kernel(tokens, gain, cot, blocks, whole, inverse, far, third, far_own):
    count, rows, part = blocks.shape
    width = tokens.shape[1]
    chunk = 64
    gains = gain_row(gain)

    @pl.loop(0, rows // chunk)
    def _(i):
        here = pl.ds(pl.multiple_of(i * chunk, chunk), chunk)
        x = tokens[here, :].astype(jnp.float32)
        inv = lax.rsqrt(jnp.sum(x * x, axis=1, keepdims=True) * (1.0 / width) + EPS)
        inverse[here, :] = inv
        normalized = ((x * inv) * gains).astype(jnp.bfloat16)
        whole[here, :] = normalized
        for j in range(count):
            blocks[j, here, :] = normalized[:, j * part : (j + 1) * part]

    places = ((far, 0), (third, 0), (third, part), (far_own, 0))
    for (by, column), (out, at) in zip(FIRST, places):
        grad_part(blocks[shard_at(by, column)], cot, out, at)


def second_kernel(blocks, cot, *outs):
    part = blocks.shape[2]
    places = [(out, at) for out in outs for at in range(0, out.shape[0], part)]
    for (by, column), (out, at) in zip(SECOND, places):
        grad_part(blocks[shard_at(by, column)], cot, out, at)


def pieces(part):
    half = part // 2
    return (
        (0, 0, part, 0, 0, 0),
        (1, 0, part, 0, 1, 0),
        (2, 0, part, -1, 0, 0),
        (3, 0, part, 1, 0, 0),
        (4, 0, part, -2, 0, 0),
        (4, part, part, -1, 1, 0),
        (5, 0, part, 1, 1, 0),
        (5, part, part, 2, 0, 0),
        (6, 0, part, -3, 0, 0),
        (6, part, part, -2, 1, 0),
        (7, 0, part, 2, 1, 0),
        (7, part, part, 3, 0, 0),
        (8, 0, half, 4, 0, half),
        (8, half, part, -3, 1, 0),
        (9, 0, part, 3, 1, 0),
        (9, part, half, 4, 0, 0),
        (10, 0, part, 4, 1, 0),
    )


def lay_out(gathered, whole):
    part = whole.shape[0] // 16
    for array, at, count, by, column, inner in pieces(part):
        to = pl.multiple_of(shard_at(by, column) * part + inner, 16)
        whole[pl.ds(to, count), :] = gathered[array][at : at + count, :]


def keys_kernel(normalized, *refs):
    gathered, (keys, whole) = refs[:11], refs[11:]
    lay_out(gathered, whole)
    for col in range(0, keys.shape[1], 256):
        product = jnp.dot(
            normalized[...], whole[:, col : col + 256], preferred_element_type=jnp.float32
        )
        keys[:, col : col + 256] = (product * whole.shape[0] ** (-0.5)).astype(keys.dtype)


def input_kernel(gain, inverse, cot, *refs):
    gathered, (source, out, tokens, whole, sem) = refs[:11], refs[11:]
    rows, width = tokens.shape
    copy = pltpu.make_async_copy(source, tokens, sem)
    copy.start()
    lay_out(gathered, whole)
    copy.wait()
    gains = gain_row(gain) * width ** (-0.5)
    inv = inverse[...]
    total = jnp.zeros((rows, 1), jnp.float32)
    cols = 256
    for col in range(0, width, cols):
        product = lax.dot_general(
            cot[...],
            whole[col : col + cols, :],
            (((1,), (1,)), ((), ())),
            preferred_element_type=jnp.float32,
        )
        value = product * gains[:, col : col + cols]
        out[:, col : col + cols] = value.astype(out.dtype)
        total += jnp.sum(
            value * tokens[:, col : col + cols].astype(jnp.float32), axis=1, keepdims=True
        )
    token_scale = total * inv * inv * inv * (1.0 / width)
    chunk = 64
    for at in range(0, rows, chunk):
        here = slice(at, at + chunk)
        x = tokens[here, :].astype(jnp.float32)
        upstream = out[here, :].astype(jnp.float32)
        out[here, :] = (upstream * inv[here] - x * token_scale[here]).astype(out.dtype)


def update_kernel(own, here, rising, falling, params, momentum, new_momentum, updated, sent):
    grad = own[...].astype(jnp.float32) + here[...].astype(jnp.float32)
    grad += rising[...].astype(jnp.float32) + falling[...].astype(jnp.float32)
    moved = BETA * momentum[...] + grad
    new_momentum[...] = moved
    value = params[...] - LRATE * moved
    updated[...] = value
    sent[...] = value.astype(sent.dtype)


def average_kernel(updated, peer, out):
    out[...] = 0.5 * (updated[...] + peer[...].astype(jnp.float32))


def local(tokens, gain, cotangent, params, momentum, step):
    rows, width = tokens.shape[1:]
    features = cotangent.shape[2]
    part, half = params.shape[1], params.shape[1] // 2
    which = jnp.remainder(step[0], 3)
    param_rows, tokens, cot = params[0], tokens[0], cotangent[0]
    gain = gain.reshape(width // 128, 128)
    bf16, f32 = jnp.bfloat16, jnp.float32

    def sums(*counts):
        return [((n * part, features), bf16) for n in counts]

    product = 2 * rows * part * features
    (own,) = call(cast_kernel, [param_rows], sums(1), moved=2**20)
    up1, down1, other = up(own), down(own), across(own)
    blocks, normalized, inverse, far, third, far_own = call(
        first_kernel,
        [tokens, gain, cot],
        [((16, rows, part), bf16), ((rows, width), bf16), ((rows, 1), f32)] + sums(1, 2, 1),
        flops=4 * product,
        moved=11 * 2**20,
    )
    up2, down2 = jnp.concatenate([up1, other]), jnp.concatenate([other, down1])
    far = across(far)
    up2, down2, third, blocks = lax.optimization_barrier((up2, down2, third, blocks))
    up2, down2, third = up(up2), down(down2), across(third)
    second, first, here, own3, own2, own1, own0 = call(
        second_kernel,
        [blocks, cot],
        sums(2, 2, 1, 2, 2, 2, 1),
        flops=12 * product,
        moved=11 * 2**20,
    )

    def reduced(owns, received, rising, falling, *earlier):
        plus = wide(owns[:part]) + wide(received[:part]) + wide(rising)
        minus = wide(owns[part:]) + wide(received[part:]) + wide(falling)
        return lax.optimization_barrier((narrow(plus), narrow(minus)) + earlier)[:2]

    sent = narrow(wide(far_own) + wide(far))
    rising, falling = up(sent[:half]), down(sent[half:])
    up2, down2, rising, falling = lax.optimization_barrier((up2, down2, rising, falling))
    up3, down3 = up(up2), down(down2)
    second = across(after(second, up2, down2))
    empty = jnp.zeros((half, features), bf16)
    rising, falling = jnp.concatenate([rising, empty]), jnp.concatenate([empty, falling])
    plus, minus = reduced(own3, third, rising, falling, up2, down2)
    rising, falling = up(plus), down(minus)

    up4, down4 = up(up3[half:]), down(down3[: part + half])
    first = across(after(first, up3, down3))
    plus, minus = reduced(own2, second, rising, falling, up3, down3)
    rising, falling = up(plus), down(minus)
    far_rows = jnp.concatenate([down4[part:], up4[:half]])
    far_other = across(far_rows)
    here = across(after(here, far_rows))
    plus, minus = reduced(own1, first, rising, falling, up4, down4)
    rising, falling = up(plus), down(minus)

    gathered = [own, other, up1, down1, up2, down2, up3, down3, up4, down4, far_other]
    whole = pltpu.VMEM((width, features), bf16)
    (keys,) = call(
        keys_kernel,
        [after(normalized, plus, minus)] + gathered,
        [((rows, features), bf16)],
        [whole],
        mib=22,
        flops=16 * product,
        moved=13 * 2**20,
    )
    stored = ((part, features), f32)
    new_momentum, updated, sent = call(
        update_kernel,
        [own0, here, rising, falling, param_rows, momentum[0]],
        [stored, stored] + sums(1),
        moved=6 * 2**20,
    )

    def finish(sent, gain, inverse, cot, *others, bit):
        peer = swapped(sent, bit)
        (input_gradient,) = call(
            input_kernel,
            [gain, inverse, cot, *others],
            [((rows, width), bf16)],
            [
                pltpu.VMEM((rows, width), bf16),
                whole,
                pltpu.SemaphoreType.DMA,
            ],
            1,
            mib=26,
            flops=16 * product,
            moved=16 * 2**20,
        )
        return peer, input_gradient

    peer, input_gradient = lax.switch(
        which,
        [partial(finish, bit=b) for b in range(3)],
        *(after(sent, keys), gain, inverse, cot, *gathered, tokens),
    )
    (averaged,) = call(average_kernel, [updated, peer], [stored], moved=2 * 2**20)
    return (keys[None], input_gradient[None], averaged[None], new_momentum[None])


def solution(mesh):
    split = Mesh(mesh.devices.reshape(mesh.devices.shape[0], -1, 2), ("rep",) + ROWS)
    rows = P("rep", ROWS, None)
    return jax.shard_map(
        local,
        mesh=split,
        in_specs=(rows, P(), rows, rows, rows, P()),
        out_specs=(rows,) * 4,
        check_vma=False,
    )
```

```python
from functools import partial

import jax
import jax.numpy as jnp
from jax import lax
from jax.experimental import pallas as pl
from jax.experimental.pallas import tpu as pltpu
from jax.sharding import Mesh, PartitionSpec as P

BETA = 0.9
LRATE = 0.1
EPS = 1e-06
ROWS = ("z", "y")
FIRST = ((4, 1), (3, 1), (-3, 1), (4, 0))
SECOND = ((2, 1), (-2, 1), (1, 1), (-1, 1), (0, 1))
SECOND += ((3, 0), (-3, 0), (2, 0), (-2, 0), (1, 0), (-1, 0), (0, 0))


def ring(n, by):
    return [(i, (i + by) % n) for i in range(n)]


def up(value):
    return lax.ppermute(value, "z", ring(lax.axis_size("z"), 1))


def down(value):
    return lax.ppermute(value, "z", ring(lax.axis_size("z"), -1))


def across(value):
    return lax.ppermute(value, "y", [(0, 1), (1, 0)])


def swapped(value, bit):
    mask = 2**bit
    pairs = [(source, source ^ mask) for source in range(lax.axis_size("rep"))]
    return lax.ppermute(value, "rep", pairs)


def after(value, *others):
    return lax.optimization_barrier((value,) + others)[0]


def wide(value):
    return value.astype(jnp.float32)


def narrow(value):
    return value.astype(jnp.bfloat16)


def shard_at(by, column):
    z, y = lax.axis_index("z"), lax.axis_index("y")
    return 2 * lax.rem(z + (by + 8), 8) + lax.rem(y + column, 2)


def call(kernel, inputs, out_shape, scratch=(), anywhere=0, mib=16, flops=0, moved=0):
    vmem = pl.BlockSpec(memory_space=pltpu.VMEM)
    free = pl.BlockSpec(memory_space=pl.ANY)
    return pl.pallas_call(
        kernel,
        in_specs=[vmem] * (len(inputs) - anywhere) + [free] * anywhere,
        out_specs=[vmem] * len(out_shape),
        out_shape=[jax.ShapeDtypeStruct(shape, dtype) for shape, dtype in out_shape],
        scratch_shapes=list(scratch),
        compiler_params=pltpu.CompilerParams(vmem_limit_bytes=mib * 2**20),
        cost_estimate=pl.CostEstimate(flops=flops, bytes_accessed=moved, transcendentals=0),
    )(*inputs)


def cast_kernel(params, out):
    out[...] = params[...].astype(out.dtype)


def gain_row(gain):
    return jnp.concatenate([gain[i : i + 1, :] for i in range(gain.shape[0])], axis=1)


def grad_part(block, cot, out, at):
    part, features = block.shape[1], cot.shape[1]
    scale = (16 * part) ** (-0.5)
    for col in range(0, features, 256):
        product = lax.dot_general(
            block,
            cot[:, col : col + 256],
            (((0,), (0,)), ((), ())),
            preferred_element_type=jnp.float32,
        )
        out[at : at + part, col : col + 256] = (product * scale).astype(out.dtype)


def first_kernel(tokens, gain, cot, blocks, inverse, far, third, far_own):
    count, rows, part = blocks.shape
    width = tokens.shape[1]
    chunk = 64
    gains = gain_row(gain)

    @pl.loop(0, rows // chunk)
    def _(i):
        here = pl.ds(pl.multiple_of(i * chunk, chunk), chunk)
        x = tokens[here, :].astype(jnp.float32)
        inv = lax.rsqrt(jnp.sum(x * x, axis=1, keepdims=True) * (1.0 / width) + EPS)
        inverse[here, :] = inv
        normalized = ((x * inv) * gains).astype(jnp.bfloat16)
        for j in range(count):
            blocks[j, here, :] = normalized[:, j * part : (j + 1) * part]

    places = ((far, 0), (third, 0), (third, part), (far_own, 0))
    for (by, column), (out, at) in zip(FIRST, places):
        grad_part(blocks[shard_at(by, column)], cot, out, at)


def second_kernel(blocks, cot, *outs):
    part = blocks.shape[2]
    places = [(out, at) for out in outs for at in range(0, out.shape[0], part)]
    for (by, column), (out, at) in zip(SECOND, places):
        grad_part(blocks[shard_at(by, column)], cot, out, at)


def pieces(part):
    half = part // 2
    return (
        (0, 0, part, 0, 0, 0),
        (1, 0, part, 0, 1, 0),
        (2, 0, part, -1, 0, 0),
        (3, 0, part, 1, 0, 0),
        (4, 0, part, -2, 0, 0),
        (4, part, part, -1, 1, 0),
        (5, 0, part, 1, 1, 0),
        (5, part, part, 2, 0, 0),
        (6, 0, part, -3, 0, 0),
        (6, part, part, -2, 1, 0),
        (7, 0, part, 2, 1, 0),
        (7, part, part, 3, 0, 0),
        (8, 0, half, 4, 0, half),
        (8, half, part, -3, 1, 0),
        (9, 0, part, 3, 1, 0),
        (9, part, half, 4, 0, 0),
        (10, 0, part, 4, 1, 0),
    )


def lay_out(gathered, whole):
    part = whole.shape[0] // 16
    for array, at, count, by, column, inner in pieces(part):
        to = pl.multiple_of(shard_at(by, column) * part + inner, 16)
        whole[pl.ds(to, count), :] = gathered[array][at : at + count, :]


def keys_kernel(tokens, gain, inverse, *refs):
    gathered, (keys, whole, normalized, sems) = refs[:11], refs[11:]
    rows, width = tokens.shape
    part = width // 16
    copies = []
    for i, (array, at, count, by, column, inner) in enumerate(pieces(part)):
        to = pl.multiple_of(shard_at(by, column) * part + inner, 16)
        copies.append(
            pltpu.make_async_copy(
                gathered[array].at[pl.ds(at, count), :], whole.at[pl.ds(to, count), :], sems.at[i]
            )
        )
    for copy in copies:
        copy.start()
    chunk = 64
    gains = gain_row(gain)

    @pl.loop(0, rows // chunk)
    def _(i):
        here = pl.ds(pl.multiple_of(i * chunk, chunk), chunk)
        x = tokens[here, :].astype(jnp.float32)
        normalized[here, :] = ((x * inverse[here, :]) * gains).astype(jnp.bfloat16)

    for copy in copies:
        copy.wait()
    for col in range(0, keys.shape[1], 256):
        product = jnp.dot(
            normalized[...], whole[:, col : col + 256], preferred_element_type=jnp.float32
        )
        keys[:, col : col + 256] = (product * width ** (-0.5)).astype(keys.dtype)


def input_kernel(gain, inverse, cot, tokens, *refs):
    gathered, (out, whole) = refs[:11], refs[11:]
    rows, width = tokens.shape
    lay_out(gathered, whole)
    gains = gain_row(gain) * width ** (-0.5)
    inv = inverse[...]
    total = jnp.zeros((rows, 1), jnp.float32)
    cols = 256
    for col in range(0, width, cols):
        product = lax.dot_general(
            cot[...],
            whole[col : col + cols, :],
            (((1,), (1,)), ((), ())),
            preferred_element_type=jnp.float32,
        )
        value = product * gains[:, col : col + cols]
        out[:, col : col + cols] = value.astype(out.dtype)
        total += jnp.sum(
            value * tokens[:, col : col + cols].astype(jnp.float32), axis=1, keepdims=True
        )
    token_scale = total * inv * inv * inv * (1.0 / width)
    chunk = 64
    for at in range(0, rows, chunk):
        here = slice(at, at + chunk)
        x = tokens[here, :].astype(jnp.float32)
        upstream = out[here, :].astype(jnp.float32)
        out[here, :] = (upstream * inv[here] - x * token_scale[here]).astype(out.dtype)


def update_kernel(own, here, rising, falling, params, momentum, new_momentum, updated, sent):
    grad = own[...].astype(jnp.float32) + here[...].astype(jnp.float32)
    grad += rising[...].astype(jnp.float32) + falling[...].astype(jnp.float32)
    moved = BETA * momentum[...] + grad
    new_momentum[...] = moved
    value = params[...] - LRATE * moved
    updated[...] = value
    sent[...] = value.astype(sent.dtype)


def average_kernel(updated, peer, out):
    out[...] = 0.5 * (updated[...] + peer[...].astype(jnp.float32))


def local(tokens, gain, cotangent, params, momentum, step):
    rows, width = tokens.shape[1:]
    features = cotangent.shape[2]
    part, half = params.shape[1], params.shape[1] // 2
    which = jnp.remainder(step[0], 3)
    param_rows, tokens, cot = params[0], tokens[0], cotangent[0]
    gain = gain.reshape(width // 128, 128)
    bf16, f32 = jnp.bfloat16, jnp.float32

    def sums(*counts):
        return [((n * part, features), bf16) for n in counts]

    product = 2 * rows * part * features
    (own,) = call(cast_kernel, [param_rows], sums(1), moved=2**20)
    up1, down1, other = up(own), down(own), across(own)
    blocks, inverse, far, third, far_own = call(
        first_kernel,
        [tokens, gain, cot],
        [((16, rows, part), bf16), ((rows, 1), f32)] + sums(1, 2, 1),
        flops=4 * product,
        moved=11 * 2**20,
    )
    up2, down2 = jnp.concatenate([up1, other]), jnp.concatenate([other, down1])
    far = across(far)
    up2, down2, third = lax.optimization_barrier((up2, down2, third))
    up2, down2, third = up(up2), down(down2), across(third)
    sent = narrow(wide(far_own) + wide(far))
    sent, blocks = lax.optimization_barrier((sent, blocks))
    rising, falling = up(sent[:half]), down(sent[half:])
    second, first, here, own3, own2, own1, own0 = call(
        second_kernel,
        [blocks, cot],
        sums(2, 2, 1, 2, 2, 2, 1),
        flops=12 * product,
        moved=11 * 2**20,
    )

    def reduced(owns, received, rising, falling, *earlier):
        plus = wide(owns[:part]) + wide(received[:part]) + wide(rising)
        minus = wide(owns[part:]) + wide(received[part:]) + wide(falling)
        return lax.optimization_barrier((narrow(plus), narrow(minus)) + earlier)[:2]

    up2, down2, rising, falling, second = lax.optimization_barrier(
        (up2, down2, rising, falling, second)
    )
    up3, down3 = up(up2), down(down2)
    second = across(after(second, up2, down2))
    empty = jnp.zeros((half, features), bf16)
    rising, falling = jnp.concatenate([rising, empty]), jnp.concatenate([empty, falling])
    plus, minus = reduced(own3, third, rising, falling, up2, down2)
    rising, falling = up(plus), down(minus)

    up4, down4 = up(up3[half:]), down(down3[: part + half])
    first = across(after(first, up3, down3))
    plus, minus = reduced(own2, second, rising, falling, up3, down3)
    rising, falling = up(plus), down(minus)
    here = across(after(here, plus, minus))
    far_rows = jnp.concatenate([down4[part:], up4[:half]])
    far_other = across(far_rows)
    plus, minus = reduced(own1, first, rising, falling, up4, down4, here)
    rising, falling = up(plus), down(minus)

    gathered = [own, other, up1, down1, up2, down2, up3, down3, up4, down4, far_other]
    whole = pltpu.VMEM((width, features), bf16)
    (keys,) = call(
        keys_kernel,
        [after(tokens, plus, minus), gain, inverse] + gathered,
        [((rows, features), bf16)],
        [whole, pltpu.VMEM((rows, width), bf16), pltpu.SemaphoreType.DMA((17,))],
        11,
        mib=20,
        flops=16 * product,
        moved=13 * 2**20,
    )
    stored = ((part, features), f32)
    new_momentum, updated, sent = call(
        update_kernel,
        [own0, here, rising, falling, param_rows, momentum[0]],
        [stored, stored] + sums(1),
        moved=6 * 2**20,
    )

    def finish(sent, *others, bit):
        peer = swapped(sent, bit)
        (input_gradient,) = call(
            input_kernel,
            others,
            [((rows, width), bf16)],
            [whole],
            mib=26,
            flops=16 * product,
            moved=16 * 2**20,
        )
        return peer, input_gradient

    peer, input_gradient = lax.switch(
        which,
        [partial(finish, bit=b) for b in range(3)],
        *(after(sent, keys), gain, inverse, cot, tokens, *gathered),
    )
    (averaged,) = call(average_kernel, [updated, peer], [stored], moved=2 * 2**20)
    return (keys[None], input_gradient[None], averaged[None], new_momentum[None])


def solution(mesh):
    split = Mesh(mesh.devices.reshape(mesh.devices.shape[0], -1, 2), ("rep",) + ROWS)
    rows = P("rep", ROWS, None)
    return jax.shard_map(
        local,
        mesh=split,
        in_specs=(rows, P(), rows, rows, rows, P()),
        out_specs=(rows,) * 4,
        check_vma=False,
    )
```

```python
from functools import partial

import jax
import jax.numpy as jnp
from jax import lax
from jax.experimental import pallas as pl
from jax.experimental.pallas import tpu as pltpu
from jax.sharding import Mesh, PartitionSpec as P

BETA = 0.9
LRATE = 0.1
EPS = 1e-06
ROWS = ("z", "y")
FIRST = ((4, 1), (3, 1), (-3, 1), (4, 0))
SECOND = ((2, 1), (-2, 1), (1, 1), (-1, 1), (0, 1))
SECOND += ((3, 0), (-3, 0), (2, 0), (-2, 0), (1, 0), (-1, 0), (0, 0))


def ring(n, by):
    return [(i, (i + by) % n) for i in range(n)]


def up(value):
    return lax.ppermute(value, "z", ring(lax.axis_size("z"), 1))


def down(value):
    return lax.ppermute(value, "z", ring(lax.axis_size("z"), -1))


def across(value):
    return lax.ppermute(value, "y", [(0, 1), (1, 0)])


def swapped(value, bit):
    mask = 2**bit
    pairs = [(source, source ^ mask) for source in range(lax.axis_size("rep"))]
    return lax.ppermute(value, "rep", pairs)


def after(value, *others):
    return lax.optimization_barrier((value,) + others)[0]


def wide(value):
    return value.astype(jnp.float32)


def narrow(value):
    return value.astype(jnp.bfloat16)


def shard_at(by, column):
    z, y = lax.axis_index("z"), lax.axis_index("y")
    return 2 * lax.rem(z + (by + 8), 8) + lax.rem(y + column, 2)


def call(kernel, inputs, out_shape, scratch=(), anywhere=0, mib=16, flops=0, moved=0):
    vmem = pl.BlockSpec(memory_space=pltpu.VMEM)
    free = pl.BlockSpec(memory_space=pl.ANY)
    return pl.pallas_call(
        kernel,
        in_specs=[vmem] * (len(inputs) - anywhere) + [free] * anywhere,
        out_specs=[vmem] * len(out_shape),
        out_shape=[jax.ShapeDtypeStruct(shape, dtype) for shape, dtype in out_shape],
        scratch_shapes=list(scratch),
        compiler_params=pltpu.CompilerParams(vmem_limit_bytes=mib * 2**20),
        cost_estimate=pl.CostEstimate(flops=flops, bytes_accessed=moved, transcendentals=0),
    )(*inputs)


def cast_kernel(params, out):
    out[...] = params[...].astype(out.dtype)


def gain_row(gain):
    return jnp.concatenate([gain[i : i + 1, :] for i in range(gain.shape[0])], axis=1)


def grad_part(block, cot, out, at):
    part, features = block.shape[1], cot.shape[1]
    scale = (16 * part) ** (-0.5)
    for col in range(0, features, 256):
        product = lax.dot_general(
            block,
            cot[:, col : col + 256],
            (((0,), (0,)), ((), ())),
            preferred_element_type=jnp.float32,
        )
        out[at : at + part, col : col + 256] = (product * scale).astype(out.dtype)


def first_kernel(tokens, gain, cot, blocks, inverse, far, third, far_own):
    count, rows, part = blocks.shape
    width = tokens.shape[1]
    chunk = 64
    gains = gain_row(gain)

    @pl.loop(0, rows // chunk)
    def _(i):
        here = pl.ds(pl.multiple_of(i * chunk, chunk), chunk)
        x = tokens[here, :].astype(jnp.float32)
        inv = lax.rsqrt(jnp.sum(x * x, axis=1, keepdims=True) * (1.0 / width) + EPS)
        inverse[here, :] = inv
        normalized = ((x * inv) * gains).astype(jnp.bfloat16)
        for j in range(count):
            blocks[j, here, :] = normalized[:, j * part : (j + 1) * part]

    places = ((far, 0), (third, 0), (third, part), (far_own, 0))
    for (by, column), (out, at) in zip(FIRST, places):
        grad_part(blocks[shard_at(by, column)], cot, out, at)


def second_kernel(blocks, cot, *outs):
    part = blocks.shape[2]
    places = [(out, at) for out in outs for at in range(0, out.shape[0], part)]
    for (by, column), (out, at) in zip(SECOND, places):
        grad_part(blocks[shard_at(by, column)], cot, out, at)


def pieces(part):
    half = part // 2
    return (
        (0, 0, part, 0, 0, 0),
        (1, 0, part, 0, 1, 0),
        (2, 0, part, -1, 0, 0),
        (3, 0, part, 1, 0, 0),
        (4, 0, part, -2, 0, 0),
        (4, part, part, -1, 1, 0),
        (5, 0, part, 1, 1, 0),
        (5, part, part, 2, 0, 0),
        (6, 0, part, -3, 0, 0),
        (6, part, part, -2, 1, 0),
        (7, 0, part, 2, 1, 0),
        (7, part, part, 3, 0, 0),
        (8, 0, half, 4, 0, half),
        (8, half, part, -3, 1, 0),
        (9, 0, part, 3, 1, 0),
        (9, part, half, 4, 0, 0),
        (10, 0, part, 4, 1, 0),
    )


def lay_out(gathered, whole):
    part = whole.shape[0] // 16
    for array, at, count, by, column, inner in pieces(part):
        to = pl.multiple_of(shard_at(by, column) * part + inner, 16)
        whole[pl.ds(to, count), :] = gathered[array][at : at + count, :]


def add_products(blocks, shards, first, out, scale):
    part = blocks.shape[2]
    for col in range(0, out.shape[1], 256):
        total = None if first is None else first[:, col : col + 256]
        for number, rows, at in shards:
            product = jnp.dot(
                blocks[number],
                rows[at : at + part, col : col + 256],
                preferred_element_type=jnp.float32,
            )
            total = product if total is None else total + product
        out[:, col : col + 256] = (total * scale).astype(out.dtype)


def near_keys_kernel(blocks, *refs):
    gathered, out = refs[:8], refs[8]
    wanted = [piece for piece in pieces(blocks.shape[2]) if piece[0] < 8]
    shards = [(shard_at(by, column), gathered[i], at) for i, at, _, by, column, _ in wanted]
    add_products(blocks, shards, None, out, 1.0)


def far_keys_kernel(blocks, near, up4, down4, far, far_other, out):
    part = blocks.shape[2]
    shards = [
        (shard_at(-3, 1), up4, part // 2),
        (shard_at(3, 1), down4, 0),
        (shard_at(4, 0), far, 0),
        (shard_at(4, 1), far_other, 0),
    ]
    add_products(blocks, shards, near, out, (16 * part) ** (-0.5))


def input_kernel(gain, inverse, cot, tokens, *refs):
    gathered, (out, whole) = refs[:11], refs[11:]
    rows, width = tokens.shape
    lay_out(gathered, whole)
    gains = gain_row(gain) * width ** (-0.5)
    inv = inverse[...]
    total = jnp.zeros((rows, 1), jnp.float32)
    cols = 256
    for col in range(0, width, cols):
        product = lax.dot_general(
            cot[...],
            whole[col : col + cols, :],
            (((1,), (1,)), ((), ())),
            preferred_element_type=jnp.float32,
        )
        value = product * gains[:, col : col + cols]
        out[:, col : col + cols] = value.astype(out.dtype)
        total += jnp.sum(
            value * tokens[:, col : col + cols].astype(jnp.float32), axis=1, keepdims=True
        )
    token_scale = total * inv * inv * inv * (1.0 / width)
    chunk = 64
    for at in range(0, rows, chunk):
        here = slice(at, at + chunk)
        x = tokens[here, :].astype(jnp.float32)
        upstream = out[here, :].astype(jnp.float32)
        out[here, :] = (upstream * inv[here] - x * token_scale[here]).astype(out.dtype)


def update_kernel(own, first, rising, falling, params, momentum, new_momentum, updated, sent):
    part = own.shape[0]
    grad = own[...].astype(jnp.float32) + first[2 * part :, :].astype(jnp.float32)
    grad += rising[...].astype(jnp.float32) + falling[...].astype(jnp.float32)
    moved = BETA * momentum[...] + grad
    new_momentum[...] = moved
    value = params[...] - LRATE * moved
    updated[...] = value
    sent[...] = value.astype(sent.dtype)


def average_kernel(updated, peer, out):
    out[...] = 0.5 * (updated[...] + peer[...].astype(jnp.float32))


def local(tokens, gain, cotangent, params, momentum, step):
    rows, width = tokens.shape[1:]
    features = cotangent.shape[2]
    part, half = params.shape[1], params.shape[1] // 2
    which = jnp.remainder(step[0], 3)
    param_rows, tokens, cot = params[0], tokens[0], cotangent[0]
    gain = gain.reshape(width // 128, 128)
    bf16, f32 = jnp.bfloat16, jnp.float32

    def sums(*counts):
        return [((n * part, features), bf16) for n in counts]

    product = 2 * rows * part * features
    (own,) = call(cast_kernel, [param_rows], sums(1), moved=2**20)
    up1, down1, other = up(own), down(own), across(own)
    blocks, inverse, far, third, far_own = call(
        first_kernel,
        [tokens, gain, cot],
        [((16, rows, part), bf16), ((rows, 1), f32)] + sums(1, 2, 1),
        flops=4 * product,
        moved=11 * 2**20,
    )
    up2, down2 = jnp.concatenate([up1, other]), jnp.concatenate([other, down1])
    far = across(far)
    up2, down2, third = lax.optimization_barrier((up2, down2, third))
    up2, down2, third = up(up2), down(down2), across(third)
    sent = narrow(wide(far_own) + wide(far))
    sent, blocks = lax.optimization_barrier((sent, blocks))
    rising, falling = up(sent[:half]), down(sent[half:])
    second, first, own3, own2, own1, own0 = call(
        second_kernel,
        [blocks, cot],
        sums(2, 3, 2, 2, 2, 1),
        flops=12 * product,
        moved=11 * 2**20,
    )

    def reduced(owns, received, rising, falling, *earlier):
        plus = wide(owns[:part]) + wide(received[:part]) + wide(rising)
        minus = wide(owns[part:]) + wide(received[part : 2 * part]) + wide(falling)
        return lax.optimization_barrier((narrow(plus), narrow(minus)) + earlier)[:2]

    up2, down2, rising, falling, second = lax.optimization_barrier(
        (up2, down2, rising, falling, second)
    )
    up3, down3 = up(up2), down(down2)
    second = across(after(second, up2, down2))
    empty = jnp.zeros((half, features), bf16)
    rising, falling = jnp.concatenate([rising, empty]), jnp.concatenate([empty, falling])
    plus, minus = reduced(own3, third, rising, falling, up2, down2)
    rising, falling = up(plus), down(minus)

    up4, down4 = up(up3[half:]), down(down3[: part + half])
    first = across(after(first, up3, down3))
    plus, minus = reduced(own2, second, rising, falling, up3, down3)
    rising, falling = up(plus), down(minus)
    blocks = after(blocks, plus, minus)
    (near,) = call(
        near_keys_kernel,
        [blocks, own, other, up1, down1, up2, down2, up3, down3],
        [((rows, features), f32)],
        flops=12 * product,
        moved=12 * 2**20,
    )
    far_rows = after(jnp.concatenate([down4[part:], up4[:half]]), near)
    far_other = across(far_rows)
    plus, minus = reduced(own1, first, rising, falling, up4, down4)
    rising, falling = up(plus), down(minus)

    (keys,) = call(
        far_keys_kernel,
        [after(blocks, plus, minus), near, up4, down4, far_rows, far_other],
        [((rows, features), bf16)],
        flops=4 * product,
        moved=9 * 2**20,
    )
    gathered = [own, other, up1, down1, up2, down2, up3, down3, up4, down4, far_other]
    (input_gradient,) = call(
        input_kernel,
        [gain, inverse, cot, after(tokens, plus, minus)] + gathered,
        [((rows, width), bf16)],
        [pltpu.VMEM((width, features), bf16)],
        mib=26,
        flops=16 * product,
        moved=16 * 2**20,
    )
    stored = ((part, features), f32)
    new_momentum, updated, sent = call(
        update_kernel,
        [own0, first, rising, falling, param_rows, momentum[0]],
        [stored, stored] + sums(1),
        moved=6 * 2**20,
    )

    peer = lax.switch(
        which, [partial(swapped, bit=b) for b in range(3)], after(sent, keys, input_gradient)
    )
    (averaged,) = call(average_kernel, [updated, peer], [stored], moved=2 * 2**20)
    return (keys[None], input_gradient[None], averaged[None], new_momentum[None])


def solution(mesh):
    split = Mesh(mesh.devices.reshape(mesh.devices.shape[0], -1, 2), ("rep",) + ROWS)
    rows = P("rep", ROWS, None)
    return jax.shard_map(
        local,
        mesh=split,
        in_specs=(rows, P(), rows, rows, rows, P()),
        out_specs=(rows,) * 4,
        check_vma=False,
    )
```

```python
from functools import partial

import jax
import jax.numpy as jnp
from jax import lax
from jax.experimental import pallas as pl
from jax.experimental.pallas import tpu as pltpu
from jax.sharding import Mesh, PartitionSpec as P

BETA = 0.9
LRATE = 0.1
EPS = 1e-06
ROWS = ("z", "y")
FIRST = ((4, 1), (3, 1), (-3, 1), (4, 0))
SECOND = ((2, 1), (-2, 1), (1, 1), (-1, 1), (0, 1))
SECOND += ((3, 0), (-3, 0), (2, 0), (-2, 0), (1, 0), (-1, 0), (0, 0))


def ring(n, by):
    return [(i, (i + by) % n) for i in range(n)]


def up(value):
    return lax.ppermute(value, "z", ring(lax.axis_size("z"), 1))


def down(value):
    return lax.ppermute(value, "z", ring(lax.axis_size("z"), -1))


def across(value):
    return lax.ppermute(value, "y", [(0, 1), (1, 0)])


def swapped(value, bit):
    mask = 2**bit
    pairs = [(source, source ^ mask) for source in range(lax.axis_size("rep"))]
    return lax.ppermute(value, "rep", pairs)


def after(value, *others):
    return lax.optimization_barrier((value,) + others)[0]


def wide(value):
    return value.astype(jnp.float32)


def narrow(value):
    return value.astype(jnp.bfloat16)


def shard_at(by, column):
    z, y = lax.axis_index("z"), lax.axis_index("y")
    return 2 * lax.rem(z + (by + 8), 8) + lax.rem(y + column, 2)


def call(kernel, inputs, out_shape, scratch=(), anywhere=0, mib=16, flops=0, moved=0):
    vmem = pl.BlockSpec(memory_space=pltpu.VMEM)
    free = pl.BlockSpec(memory_space=pl.ANY)
    return pl.pallas_call(
        kernel,
        in_specs=[vmem] * (len(inputs) - anywhere) + [free] * anywhere,
        out_specs=[vmem] * len(out_shape),
        out_shape=[jax.ShapeDtypeStruct(shape, dtype) for shape, dtype in out_shape],
        scratch_shapes=list(scratch),
        compiler_params=pltpu.CompilerParams(vmem_limit_bytes=mib * 2**20),
        cost_estimate=pl.CostEstimate(flops=flops, bytes_accessed=moved, transcendentals=0),
    )(*inputs)


def cast_kernel(params, out):
    out[...] = params[...].astype(out.dtype)


def gain_row(gain):
    return jnp.concatenate([gain[i : i + 1, :] for i in range(gain.shape[0])], axis=1)


def grad_part(block, cot, out, at):
    part, features = block.shape[1], cot.shape[1]
    scale = (16 * part) ** (-0.5)
    for col in range(0, features, 256):
        product = lax.dot_general(
            block,
            cot[:, col : col + 256],
            (((0,), (0,)), ((), ())),
            preferred_element_type=jnp.float32,
        )
        out[at : at + part, col : col + 256] = (product * scale).astype(out.dtype)


def first_kernel(tokens, gain, cot, blocks, inverse, far, third, far_own):
    count, rows, part = blocks.shape
    width = tokens.shape[1]
    chunk = 64
    gains = gain_row(gain)

    @pl.loop(0, rows // chunk)
    def _(i):
        here = pl.ds(pl.multiple_of(i * chunk, chunk), chunk)
        x = tokens[here, :].astype(jnp.float32)
        inv = lax.rsqrt(jnp.sum(x * x, axis=1, keepdims=True) * (1.0 / width) + EPS)
        inverse[here, :] = inv
        normalized = ((x * inv) * gains).astype(jnp.bfloat16)
        for j in range(count):
            blocks[j, here, :] = normalized[:, j * part : (j + 1) * part]

    places = ((far, 0), (third, 0), (third, part), (far_own, 0))
    for (by, column), (out, at) in zip(FIRST, places):
        grad_part(blocks[shard_at(by, column)], cot, out, at)


def second_kernel(blocks, cot, *outs):
    part = blocks.shape[2]
    places = [(out, at) for out in outs for at in range(0, out.shape[0], part)]
    for (by, column), (out, at) in zip(SECOND, places):
        grad_part(blocks[shard_at(by, column)], cot, out, at)


def pieces(part):
    half = part // 2
    return (
        (0, 0, part, 0, 0, 0),
        (1, 0, part, 0, 1, 0),
        (2, 0, part, -1, 0, 0),
        (3, 0, part, 1, 0, 0),
        (4, 0, part, -2, 0, 0),
        (4, part, part, -1, 1, 0),
        (5, 0, part, 1, 1, 0),
        (5, part, part, 2, 0, 0),
        (6, 0, part, -3, 0, 0),
        (6, part, part, -2, 1, 0),
        (7, 0, part, 2, 1, 0),
        (7, part, part, 3, 0, 0),
        (8, 0, half, 4, 0, half),
        (8, half, part, -3, 1, 0),
        (9, 0, part, 3, 1, 0),
        (9, part, half, 4, 0, 0),
        (10, 0, part, 4, 1, 0),
    )


def near_keys_kernel(blocks, *refs):
    gathered, out = refs[:8], refs[8]
    part = blocks.shape[2]
    wanted = [piece for piece in pieces(part) if piece[0] < 8]
    for col in range(0, out.shape[1], 256):
        total = None
        for array, at, _, by, column, _ in wanted:
            product = jnp.dot(
                blocks[shard_at(by, column)],
                gathered[array][at : at + part, col : col + 256],
                preferred_element_type=jnp.float32,
            )
            total = product if total is None else total + product
        out[:, col : col + 256] = total


def last_kernel(gain, inverse, *refs):
    (tokens_far, cot_far, blocks_far, near_far), gathered = refs[:4], refs[4:15]
    keys, out, whole, tokens, cot, blocks, near, sems = refs[15:]
    rows, width = tokens.shape
    part = width // 16
    shards = [shard_at(by, column) for by, column in ((-3, 1), (3, 1), (4, 0), (4, 1))]
    pairs = [(near_far, near)]
    pairs += [(blocks_far.at[number], blocks.at[i]) for i, number in enumerate(shards)]
    early = len(pairs) + 5
    for array, at, count, by, column, inner in sorted(pieces(part), key=lambda p: p[0] < 8):
        to = pl.multiple_of(shard_at(by, column) * part + inner, 16)
        pairs.append((gathered[array].at[pl.ds(at, count), :], whole.at[pl.ds(to, count), :]))
    pairs += [(cot_far, cot), (tokens_far, tokens)]
    copies = [pltpu.make_async_copy(*pair, sems.at[i]) for i, pair in enumerate(pairs)]
    for copy in copies:
        copy.start()
    gains = gain_row(gain) * width ** (-0.5)
    inv = inverse[...]
    for copy in copies[:early]:
        copy.wait()
    cols = 256
    for col in range(0, keys.shape[1], cols):
        total = near[:, col : col + cols]
        for i, number in enumerate(shards):
            at = pl.multiple_of(number * part, 16)
            total += jnp.dot(
                blocks[i],
                whole[pl.ds(at, part), col : col + cols],
                preferred_element_type=jnp.float32,
            )
        keys[:, col : col + cols] = (total * width ** (-0.5)).astype(keys.dtype)
    for copy in copies[early:]:
        copy.wait()
    total = jnp.zeros((rows, 1), jnp.float32)
    for col in range(0, width, cols):
        product = lax.dot_general(
            cot[...],
            whole[col : col + cols, :],
            (((1,), (1,)), ((), ())),
            preferred_element_type=jnp.float32,
        )
        value = product * gains[:, col : col + cols]
        out[:, col : col + cols] = value.astype(out.dtype)
        total += jnp.sum(
            value * tokens[:, col : col + cols].astype(jnp.float32), axis=1, keepdims=True
        )
    token_scale = total * inv * inv * inv * (1.0 / width)
    chunk = 64
    for at in range(0, rows, chunk):
        here = slice(at, at + chunk)
        x = tokens[here, :].astype(jnp.float32)
        upstream = out[here, :].astype(jnp.float32)
        out[here, :] = (upstream * inv[here] - x * token_scale[here]).astype(out.dtype)


def update_kernel(own, first, rising, falling, params, momentum, new_momentum, updated, sent):
    part = own.shape[0]
    grad = own[...].astype(jnp.float32) + first[2 * part :, :].astype(jnp.float32)
    grad += rising[...].astype(jnp.float32) + falling[...].astype(jnp.float32)
    moved = BETA * momentum[...] + grad
    new_momentum[...] = moved
    value = params[...] - LRATE * moved
    updated[...] = value
    sent[...] = value.astype(sent.dtype)


def average_kernel(updated, peer, out):
    out[...] = 0.5 * (updated[...] + peer[...].astype(jnp.float32))


def local(tokens, gain, cotangent, params, momentum, step):
    rows, width = tokens.shape[1:]
    features = cotangent.shape[2]
    part, half = params.shape[1], params.shape[1] // 2
    which = jnp.remainder(step[0], 3)
    param_rows, tokens, cot = params[0], tokens[0], cotangent[0]
    gain = gain.reshape(width // 128, 128)
    bf16, f32 = jnp.bfloat16, jnp.float32

    def sums(*counts):
        return [((n * part, features), bf16) for n in counts]

    product = 2 * rows * part * features
    (own,) = call(cast_kernel, [param_rows], sums(1), moved=2**20)
    up1, down1, other = up(own), down(own), across(own)
    blocks, inverse, far, third, far_own = call(
        first_kernel,
        [tokens, gain, cot],
        [((16, rows, part), bf16), ((rows, 1), f32)] + sums(1, 2, 1),
        flops=4 * product,
        moved=11 * 2**20,
    )
    up2, down2 = jnp.concatenate([up1, other]), jnp.concatenate([other, down1])
    far = across(far)
    up2, down2, third = lax.optimization_barrier((up2, down2, third))
    up2, down2, third = up(up2), down(down2), across(third)
    sent = narrow(wide(far_own) + wide(far))
    sent, blocks = lax.optimization_barrier((sent, blocks))
    rising, falling = up(sent[:half]), down(sent[half:])
    second, first, own3, own2, own1, own0 = call(
        second_kernel,
        [blocks, cot],
        sums(2, 3, 2, 2, 2, 1),
        flops=12 * product,
        moved=11 * 2**20,
    )

    def reduced(owns, received, rising, falling, *earlier):
        plus = wide(owns[:part]) + wide(received[:part]) + wide(rising)
        minus = wide(owns[part:]) + wide(received[part : 2 * part]) + wide(falling)
        return lax.optimization_barrier((narrow(plus), narrow(minus)) + earlier)[:2]

    up2, down2, rising, falling, second = lax.optimization_barrier(
        (up2, down2, rising, falling, second)
    )
    up3, down3 = up(up2), down(down2)
    second = across(after(second, up2, down2))
    empty = jnp.zeros((half, features), bf16)
    rising, falling = jnp.concatenate([rising, empty]), jnp.concatenate([empty, falling])
    plus, minus = reduced(own3, third, rising, falling, up2, down2)
    rising, falling = up(plus), down(minus)

    up4, down4 = up(up3[half:]), down(down3[: part + half])
    first = across(after(first, up3, down3))
    plus, minus = reduced(own2, second, rising, falling, up3, down3)
    rising, falling = up(plus), down(minus)
    blocks = after(blocks, plus, minus)
    (near,) = call(
        near_keys_kernel,
        [blocks, own, other, up1, down1, up2, down2, up3, down3],
        [((rows, features), f32)],
        flops=12 * product,
        moved=12 * 2**20,
    )
    far_rows = after(jnp.concatenate([down4[part:], up4[:half]]), near)
    far_other = across(far_rows)
    plus, minus = reduced(own1, first, rising, falling, up4, down4)
    rising, falling = up(plus), down(minus)

    gathered = [own, other, up1, down1, up2, down2, up3, down3, up4, down4, far_other]
    keys, input_gradient = call(
        last_kernel,
        [gain, inverse, tokens, cot, after(blocks, plus, minus), near] + gathered,
        [((rows, features), bf16), ((rows, width), bf16)],
        [
            pltpu.VMEM((width, features), bf16),
            pltpu.VMEM((rows, width), bf16),
            pltpu.VMEM((rows, features), bf16),
            pltpu.VMEM((4, rows, part), bf16),
            pltpu.VMEM((rows, features), f32),
            pltpu.SemaphoreType.DMA((24,)),
        ],
        15,
        mib=34,
        flops=20 * product,
        moved=20 * 2**20,
    )
    stored = ((part, features), f32)
    new_momentum, updated, sent = call(
        update_kernel,
        [own0, first, rising, falling, param_rows, momentum[0]],
        [stored, stored] + sums(1),
        moved=6 * 2**20,
    )

    peer = lax.switch(
        which, [partial(swapped, bit=b) for b in range(3)], after(sent, keys, input_gradient)
    )
    (averaged,) = call(average_kernel, [updated, peer], [stored], moved=2 * 2**20)
    return (keys[None], input_gradient[None], averaged[None], new_momentum[None])


def solution(mesh):
    split = Mesh(mesh.devices.reshape(mesh.devices.shape[0], -1, 2), ("rep",) + ROWS)
    rows = P("rep", ROWS, None)
    return jax.shard_map(
        local,
        mesh=split,
        in_specs=(rows, P(), rows, rows, rows, P()),
        out_specs=(rows,) * 4,
        check_vma=False,
    )
```

```python
from functools import partial

import jax
import jax.numpy as jnp
from jax import lax
from jax.experimental import pallas as pl
from jax.experimental.pallas import tpu as pltpu
from jax.sharding import Mesh, PartitionSpec as P

BETA = 0.9
LRATE = 0.1
EPS = 1e-06
ROWS = ("z", "y")
FIRST = ((4, 1), (3, 1), (-3, 1), (4, 0))
SECOND = ((2, 1), (-2, 1), (1, 1), (-1, 1), (0, 1))
SECOND += ((3, 0), (-3, 0), (2, 0), (-2, 0), (1, 0), (-1, 0), (0, 0))


LAST = ((-3, 1), (3, 1), (4, 0), (4, 1))


def ring(n, by):
    return [(i, (i + by) % n) for i in range(n)]


def up(value):
    return lax.ppermute(value, "z", ring(lax.axis_size("z"), 1))


def down(value):
    return lax.ppermute(value, "z", ring(lax.axis_size("z"), -1))


def across(value):
    return lax.ppermute(value, "y", [(0, 1), (1, 0)])


def swapped(value, bit):
    mask = 2**bit
    pairs = [(source, source ^ mask) for source in range(lax.axis_size("rep"))]
    return lax.ppermute(value, "rep", pairs)


def after(value, *others):
    return lax.optimization_barrier((value,) + others)[0]


def wide(value):
    return value.astype(jnp.float32)


def narrow(value):
    return value.astype(jnp.bfloat16)


def shard_at(by, column):
    z, y = lax.axis_index("z"), lax.axis_index("y")
    return 2 * lax.rem(z + (by + 8), 8) + lax.rem(y + column, 2)


def call(kernel, inputs, out_shape, scratch=(), anywhere=0, mib=16, flops=0, moved=0):
    vmem = pl.BlockSpec(memory_space=pltpu.VMEM)
    free = pl.BlockSpec(memory_space=pl.ANY)
    return pl.pallas_call(
        kernel,
        in_specs=[vmem] * (len(inputs) - anywhere) + [free] * anywhere,
        out_specs=[vmem] * len(out_shape),
        out_shape=[jax.ShapeDtypeStruct(shape, dtype) for shape, dtype in out_shape],
        scratch_shapes=list(scratch),
        compiler_params=pltpu.CompilerParams(vmem_limit_bytes=mib * 2**20),
        cost_estimate=pl.CostEstimate(flops=flops, bytes_accessed=moved, transcendentals=0),
    )(*inputs)


def cast_kernel(params, out):
    out[...] = params[...].astype(out.dtype)


def gain_row(gain):
    return jnp.concatenate([gain[i : i + 1, :] for i in range(gain.shape[0])], axis=1)


def grad_part(block, cot, out, at):
    part, features = block.shape[1], cot.shape[1]
    scale = (16 * part) ** (-0.5)
    for col in range(0, features, 256):
        product = lax.dot_general(
            block,
            cot[:, col : col + 256],
            (((0,), (0,)), ((), ())),
            preferred_element_type=jnp.float32,
        )
        out[at : at + part, col : col + 256] = (product * scale).astype(out.dtype)


def first_kernel(tokens, gain, cot, blocks, inverse, far, third, far_own):
    count, rows, part = blocks.shape
    width = tokens.shape[1]
    chunk = 64
    gains = gain_row(gain)

    @pl.loop(0, rows // chunk)
    def _(i):
        here = pl.ds(pl.multiple_of(i * chunk, chunk), chunk)
        x = tokens[here, :].astype(jnp.float32)
        inv = lax.rsqrt(jnp.sum(x * x, axis=1, keepdims=True) * (1.0 / width) + EPS)
        inverse[here, :] = inv
        normalized = ((x * inv) * gains).astype(jnp.bfloat16)
        for j in range(count):
            blocks[j, here, :] = normalized[:, j * part : (j + 1) * part]

    places = ((far, 0), (third, 0), (third, part), (far_own, 0))
    for (by, column), (out, at) in zip(FIRST, places):
        grad_part(blocks[shard_at(by, column)], cot, out, at)


def second_kernel(blocks, cot, *outs):
    part = blocks.shape[2]
    places = [(out, at) for out in outs for at in range(0, out.shape[0], part)]
    for (by, column), (out, at) in zip(SECOND, places):
        grad_part(blocks[shard_at(by, column)], cot, out, at)


def pieces(part):
    half = part // 2
    return (
        (0, 0, part, 0, 0, 0),
        (1, 0, part, 0, 1, 0),
        (2, 0, part, -1, 0, 0),
        (3, 0, part, 1, 0, 0),
        (4, 0, part, -2, 0, 0),
        (4, part, part, -1, 1, 0),
        (5, 0, part, 1, 1, 0),
        (5, part, part, 2, 0, 0),
        (6, 0, part, -3, 0, 0),
        (6, part, part, -2, 1, 0),
        (7, 0, part, 2, 1, 0),
        (7, part, part, 3, 0, 0),
        (8, 0, half, 4, 0, half),
        (8, half, part, -3, 1, 0),
        (9, 0, part, 3, 1, 0),
        (9, part, half, 4, 0, 0),
        (10, 0, part, 4, 1, 0),
    )


def lay_out(gathered, whole):
    part = whole.shape[0] // 16
    for array, at, count, by, column, inner in pieces(part):
        to = pl.multiple_of(shard_at(by, column) * part + inner, 16)
        whole[pl.ds(to, count), :] = gathered[array][at : at + count, :]


def add_products(blocks, shards, first, out, scale):
    part = blocks.shape[2]
    for col in range(0, out.shape[1], 256):
        total = None if first is None else first[:, col : col + 256]
        for number, rows, at in shards:
            product = jnp.dot(
                blocks[number],
                rows[at : at + part, col : col + 256],
                preferred_element_type=jnp.float32,
            )
            total = product if total is None else total + product
        out[:, col : col + 256] = (total * scale).astype(out.dtype)


def near_keys_kernel(blocks, *refs):
    gathered, out, kept = refs[:8], refs[8], refs[9]
    for i, (by, column) in enumerate(LAST):
        kept[i] = blocks[shard_at(by, column)]
    wanted = [piece for piece in pieces(blocks.shape[2]) if piece[0] < 8]
    shards = [(shard_at(by, column), gathered[i], at) for i, at, _, by, column, _ in wanted]
    add_products(blocks, shards, None, out, 1.0)


def far_keys_kernel(kept, near, up4, down4, far, far_other, out):
    part = kept.shape[2]
    shards = [(0, up4, part // 2), (1, down4, 0), (2, far, 0), (3, far_other, 0)]
    add_products(kept, shards, near, out, (16 * part) ** (-0.5))


def input_kernel(gain, inverse, cot, tokens, *refs):
    gathered, (out, whole) = refs[:11], refs[11:]
    rows, width = tokens.shape
    lay_out(gathered, whole)
    gains = gain_row(gain) * width ** (-0.5)
    inv = inverse[...]
    total = jnp.zeros((rows, 1), jnp.float32)
    cols = 256
    for col in range(0, width, cols):
        product = lax.dot_general(
            cot[...],
            whole[col : col + cols, :],
            (((1,), (1,)), ((), ())),
            preferred_element_type=jnp.float32,
        )
        value = product * gains[:, col : col + cols]
        out[:, col : col + cols] = value.astype(out.dtype)
        total += jnp.sum(
            value * tokens[:, col : col + cols].astype(jnp.float32), axis=1, keepdims=True
        )
    token_scale = total * inv * inv * inv * (1.0 / width)
    chunk = 64
    for at in range(0, rows, chunk):
        here = slice(at, at + chunk)
        x = tokens[here, :].astype(jnp.float32)
        upstream = out[here, :].astype(jnp.float32)
        out[here, :] = (upstream * inv[here] - x * token_scale[here]).astype(out.dtype)


def update_kernel(own, first, rising, falling, params, momentum, new_momentum, updated, sent):
    part = own.shape[0]
    grad = own[...].astype(jnp.float32) + first[2 * part :, :].astype(jnp.float32)
    grad += rising[...].astype(jnp.float32) + falling[...].astype(jnp.float32)
    moved = BETA * momentum[...] + grad
    new_momentum[...] = moved
    value = params[...] - LRATE * moved
    updated[...] = value
    sent[...] = value.astype(sent.dtype)


def average_kernel(updated, peer, out):
    out[...] = 0.5 * (updated[...] + peer[...].astype(jnp.float32))


def local(tokens, gain, cotangent, params, momentum, step):
    rows, width = tokens.shape[1:]
    features = cotangent.shape[2]
    part, half = params.shape[1], params.shape[1] // 2
    which = jnp.remainder(step[0], 3)
    param_rows, tokens, cot = params[0], tokens[0], cotangent[0]
    gain = gain.reshape(width // 128, 128)
    bf16, f32 = jnp.bfloat16, jnp.float32

    def sums(*counts):
        return [((n * part, features), bf16) for n in counts]

    product = 2 * rows * part * features
    (own,) = call(cast_kernel, [param_rows], sums(1), moved=2**20)
    up1, down1, other = up(own), down(own), across(own)
    blocks, inverse, far, third, far_own = call(
        first_kernel,
        [tokens, gain, cot],
        [((16, rows, part), bf16), ((rows, 1), f32)] + sums(1, 2, 1),
        flops=4 * product,
        moved=11 * 2**20,
    )
    up2, down2 = jnp.concatenate([up1, other]), jnp.concatenate([other, down1])
    far = across(far)
    up2, down2, third = lax.optimization_barrier((up2, down2, third))
    up2, down2, third = up(up2), down(down2), across(third)
    sent = narrow(wide(far_own) + wide(far))
    sent, blocks = lax.optimization_barrier((sent, blocks))
    rising, falling = up(sent[:half]), down(sent[half:])
    second, first, own3, own2, own1, own0 = call(
        second_kernel,
        [blocks, cot],
        sums(2, 3, 2, 2, 2, 1),
        flops=12 * product,
        moved=11 * 2**20,
    )

    def reduced(owns, received, rising, falling, *earlier):
        plus = wide(owns[:part]) + wide(received[:part]) + wide(rising)
        minus = wide(owns[part:]) + wide(received[part : 2 * part]) + wide(falling)
        return lax.optimization_barrier((narrow(plus), narrow(minus)) + earlier)[:2]

    up2, down2, rising, falling, second = lax.optimization_barrier(
        (up2, down2, rising, falling, second)
    )
    up3, down3 = up(up2), down(down2)
    second = across(after(second, up2, down2))
    empty = jnp.zeros((half, features), bf16)
    rising, falling = jnp.concatenate([rising, empty]), jnp.concatenate([empty, falling])
    plus, minus = reduced(own3, third, rising, falling, up2, down2)
    rising, falling = up(plus), down(minus)

    up4, down4 = up(up3[half:]), down(down3[: part + half])
    first = across(after(first, up3, down3))
    plus, minus = reduced(own2, second, rising, falling, up3, down3)
    rising, falling = up(plus), down(minus)
    blocks = after(blocks, plus, minus)
    near, kept = call(
        near_keys_kernel,
        [blocks, own, other, up1, down1, up2, down2, up3, down3],
        [((rows, features), f32), ((4, rows, part), bf16)],
        flops=12 * product,
        moved=12 * 2**20,
    )
    far_rows = after(jnp.concatenate([down4[part:], up4[:half]]), near)
    far_other = across(far_rows)
    plus, minus = reduced(own1, first, rising, falling, up4, down4)
    rising, falling = up(plus), down(minus)

    (keys,) = call(
        far_keys_kernel,
        [after(kept, plus, minus), near, up4, down4, far_rows, far_other],
        [((rows, features), bf16)],
        flops=4 * product,
        moved=9 * 2**20,
    )
    gathered = [own, other, up1, down1, up2, down2, up3, down3, up4, down4, far_other]
    (input_gradient,) = call(
        input_kernel,
        [gain, inverse, cot, after(tokens, plus, minus)] + gathered,
        [((rows, width), bf16)],
        [pltpu.VMEM((width, features), bf16)],
        mib=26,
        flops=16 * product,
        moved=16 * 2**20,
    )
    stored = ((part, features), f32)
    new_momentum, updated, sent = call(
        update_kernel,
        [own0, first, rising, falling, param_rows, momentum[0]],
        [stored, stored] + sums(1),
        moved=6 * 2**20,
    )

    peer = lax.switch(
        which, [partial(swapped, bit=b) for b in range(3)], after(sent, keys, input_gradient)
    )
    (averaged,) = call(average_kernel, [updated, peer], [stored], moved=2 * 2**20)
    return (keys[None], input_gradient[None], averaged[None], new_momentum[None])


def solution(mesh):
    split = Mesh(mesh.devices.reshape(mesh.devices.shape[0], -1, 2), ("rep",) + ROWS)
    rows = P("rep", ROWS, None)
    return jax.shard_map(
        local,
        mesh=split,
        in_specs=(rows, P(), rows, rows, rows, P()),
        out_specs=(rows,) * 4,
        check_vma=False,
    )
```
